32 devices in a mesh: row: 4 (over y, core), col: 8 (over z, x).
Axes of the slice: x: 2, y: 2, z: 4, core: 2. Of those that a mesh axis runs over, the one named last changes fastest.
Arguments:
- rhs_scen: bfloat16 [256, 32768], P(('row', 'col')), may hold values from -6 to 6
- factor_panels: bfloat16 [32768, 8192], P(('row', 'col')), as said below
Outputs:
- current: float32 [32768, 256], P(('row', 'col'))
The draws below stay inside these ranges and needn't reach their ends.
Inputs may be any that keep to these rules, and one draw needn't show every extreme that they name: `factor_panels`: in the rows of block b (b < 4, blocks of 2048 rows), every entry in the columns of later blocks is zero, and so is every entry above the diagonal of block b's own columns.
All inputs are finite; a program needn't handle non-finite values.
Results may differ from the reference program's by a relative error of at most 0.0023.
Values may be sent and summed in bfloat16 or wider, within the bound.
No kernel may reach another device: no remote copies, remote signals or barrier semaphores. Data moves between devices by JAX's collectives and lax.ppermute only.
A program may use at most 128 MiB of HBM per device.

```python
import math
import jax
import jax.numpy as jnp

NB = 2048
STEPS = 4
NORD = 32768
SCEN = 256


def draw_factor_panels(key, part):
    row_ids = jnp.arange(NORD, dtype=jnp.int32)[:, None]
    col_ids = jnp.arange(STEPS * NB, dtype=jnp.int32)[None, :]
    base = jax.random.truncated_normal(key, -4.0, 4.0, (NORD, STEPS * NB), jnp.float32)
    scaled = base * (0.5 / math.sqrt(NB))
    row_block = row_ids // NB
    col_block = col_ids // NB
    inner_row = row_ids % NB
    inner_col = col_ids % NB
    diag_value = 1.0 + 0.3 * jnp.tanh(base)
    within = jnp.where(inner_row == inner_col, diag_value, jnp.where(inner_row > inner_col, 1.2 * scaled, 0.0))
    return jnp.where(row_block == col_block, within, jnp.where(row_block > col_block, scaled, 0.0)).astype(jnp.bfloat16)


def levels(own_key, extent, pieces, smallest, top_value):
    def one(position, parts):
        heights = jax.random.uniform(jax.random.fold_in(jax.random.fold_in(own_key, 6), position), (parts,), jnp.float32, smallest / len(pieces), top_value / len(pieces))
        return jnp.repeat(jnp.exp(heights), extent[position] // parts).reshape((-1,) + (1,) * (len(extent) - position - 1))

    factor_of = one(*pieces[0])
    for cut in pieces[1:]:
        factor_of = factor_of * one(*cut)
    return factor_of


def noise(stream_key, extent, spread, most, split=(), held_as=jnp.bfloat16):
    factor_of = levels(stream_key, extent, split, -0.22, 0.18) if split else 1.0
    array = jax.random.normal(stream_key, extent, jnp.float32) * spread * factor_of
    return jnp.minimum(jnp.maximum(array, -most), most).astype(held_as)


def setup_inputs(seed: int = 0) -> dict:
    key_list = jax.random.split(jax.random.key(seed), 3)
    return {
        "rhs_scen": noise(key_list[0], (SCEN, NORD), 1.0, 6.0, ((0, 32),)),
        "factor_panels": draw_factor_panels(jax.random.fold_in(key_list[2], 71), 0),
    }


def reference(rhs_scen, factor_panels):
    current = jnp.transpose(rhs_scen).astype(jnp.float32)
    for block_step in range(STEPS):
        lower = block_step * NB
        outgoing = current[lower:lower + NB].astype(jnp.bfloat16)
        product = jnp.dot(factor_panels[:, lower:lower + NB], outgoing, preferred_element_type=jnp.float32)
        updated = current - product
        current = updated.at[lower:lower + NB].set(product[lower:lower + NB])
    return current
```

```python
import jax
import jax.numpy as jnp
from jax import lax
from jax.sharding import PartitionSpec as P

NB = 2048
STEPS = 4
AXES = ("row", "col")
CORES = 2


def make_on_device(n_row, n_col):
    def on_device(rhs_scen, factor_panels):
        rows_here = factor_panels.shape[0]
        lanes = NB // rows_here
        planes = n_col // lanes
        n_y = n_row // CORES
        row, col = lax.axis_index("row"), lax.axis_index("col")
        y, core = row // CORES, row % CORES
        plane, lane = col // lanes, col % lanes
        flat = row * n_col + col
        my_block = flat // lanes
        piece_rows = rows_here // n_y

        def device(y, core, plane, lane):
            return (y * CORES + core) * n_col + plane * lanes + lane

        def send(value, pairs):
            return lax.ppermute(value, AXES, pairs)

        def in_order(parts, me):
            n = len(parts)
            if n == 1:
                return parts[0]
            size = parts[0].shape[0]
            twice = jnp.concatenate(parts + parts[:-1], axis=0)
            start = ((n - me) % n) * size
            return lax.dynamic_slice_in_dim(twice, start, n * size, axis=0)

        def to_next_block(own, k):
            parts = []
            for d in range(lanes):
                pairs = [
                    (device(0, 0, k, (m + d) % lanes), device(0, 0, k + 1, m)) for m in range(lanes)
                ]
                parts.append(send(own, pairs))
            return in_order(parts, lane)

        def to_all(own, k):
            piece = own[:piece_rows]
            for t in range(1, n_y):
                cut = own[t * piece_rows : (t + 1) * piece_rows]
                pairs = [(device(0, 0, k, m), device(t, 0, k, m)) for m in range(lanes)]
                piece = jnp.where(y == t, send(cut, pairs), piece)
            held = piece
            for z in range(planes):
                if z != k:
                    pairs = [
                        (device(t, 0, k, m), device(t, 0, z, m)) for t in range(n_y) for m in range(lanes)
                    ]
                    held = jnp.where(plane == z, send(piece, pairs), held)
            members = lanes * n_y
            parts = [held]
            for d in range(1, members):
                pairs = []
                for z in range(planes):
                    for i in range(members):
                        j = (i + d) % members
                        pairs.append(
                            (device(j % n_y, 0, z, j // n_y), device(i % n_y, 0, z, i // n_y))
                        )
                parts.append(send(held, pairs))
            whole = in_order(parts, lane * n_y + y)
            pairs = [
                (device(t, 0, z, m), device(t, 1, z, m))
                for t in range(n_y) for z in range(planes) for m in range(lanes)
            ]
            return jnp.where(core == 0, whole, send(whole, pairs))

        def panel(k):
            return factor_panels[:, k * NB : (k + 1) * NB]

        first = lax.all_gather(rhs_scen[:, :NB], AXES, axis=0, tiled=True)
        regrouped = lax.all_to_all(rhs_scen, AXES, split_axis=1, concat_axis=0, tiled=True)
        rhs = jnp.transpose(regrouped).astype(jnp.float32)

        def product(k, outgoing):
            return jnp.dot(panel(k), outgoing, preferred_element_type=jnp.float32)

        products = [
            lax.dot_general(panel(0), first, (((1,), (1,)), ((), ())), preferred_element_type=jnp.float32)
        ]
        current = rhs - products[0]
        chain = current
        for k in range(1, STEPS):
            own = chain.astype(jnp.bfloat16)
            if k + 1 < STEPS:
                ahead = product(k, to_next_block(own, k))
            whole = to_all(own, k)
            products.append(product(k, whole))
            chain = current - ahead if k + 1 < STEPS else None
            current = current - products[k]
        out = current
        for k in range(STEPS):
            out = jnp.where(my_block == k, products[k], out)
        return out

    return on_device


def solution(mesh):
    placed = (P(AXES, None), P(AXES, None))
    on_device = make_on_device(mesh.shape["row"], mesh.shape["col"])
    return jax.shard_map(
        on_device, mesh=mesh, in_specs=placed, out_specs=P(AXES, None), check_vma=False
    )
```

```python
import functools

import jax
import jax.numpy as jnp
from jax import lax
from jax.experimental import pallas as pl
from jax.experimental.pallas import tpu as pltpu
from jax.sharding import PartitionSpec as P

NB = 2048
STEPS = 4
AXES = ("row", "col")
CORES = 2
TILE = 256


def after(value, *others):
    return lax.optimization_barrier((value, *others))[0]


def step_kernel(counts, n_out, *refs):
    info, current = refs[0], refs[1]
    at = 2
    panels = refs[at : at + len(counts)]
    at += len(counts)
    pieces = []
    for n in counts:
        pieces.append(refs[at : at + n])
        at += n
    outs = refs[at : at + n_out]
    held = refs[at + n_out :]

    @pl.when(pl.program_id(0) == 0)
    def _():
        place = len(counts)
        for t, n in enumerate(counts):
            for piece in pieces[t]:
                size = piece.shape[0]
                start = pl.multiple_of(info[place] * size, size)
                held[t][pl.ds(start, size), :] = piece[...]
                place += 1

    value = current[...]
    for t in range(len(counts)):
        product = jnp.dot(panels[t][...], held[t][...], preferred_element_type=jnp.float32)
        value = jnp.where(info[t] == 1, product, value - product)
    for out in outs:
        out[...] = value.astype(out.dtype)


def steps(current, factor_panels, terms, my_block, out_types):
    rows, scenarios = current.shape
    tile = min(TILE, rows)
    counts = tuple(len(pieces) for _, pieces, _ in terms)
    info = [my_block == k for k, _, _ in terms]
    for _, _, places in terms:
        info.extend(places)
    info = jnp.stack([jnp.asarray(x, jnp.int32) for x in info])
    by_tile = pl.BlockSpec((tile, scenarios), lambda i, _: (i, 0))
    specs = [by_tile]
    operands = [current]
    for k, _, _ in terms:
        specs.append(pl.BlockSpec((tile, NB), functools.partial(lambda k, i, _: (i, k), k)))
        operands.append(factor_panels)
    for _, pieces, _ in terms:
        for piece in pieces:
            specs.append(pl.BlockSpec(piece.shape, lambda i, _: (0, 0)))
            operands.append(piece)
    result = pl.pallas_call(
        functools.partial(step_kernel, counts, len(out_types)),
        grid_spec=pltpu.PrefetchScalarGridSpec(
            num_scalar_prefetch=1,
            grid=(rows // tile,),
            in_specs=specs,
            out_specs=[by_tile] * len(out_types),
            scratch_shapes=[pltpu.VMEM((NB, scenarios), jnp.bfloat16)] * len(terms),
        ),
        out_shape=[jax.ShapeDtypeStruct((rows, scenarios), t) for t in out_types],
        compiler_params=pltpu.CompilerParams(vmem_limit_bytes=50 * 1024 * 1024),
        cost_estimate=pl.CostEstimate(
            flops=2 * rows * NB * scenarios * len(terms),
            bytes_accessed=2 * rows * NB * len(terms) + 8 * rows * scenarios,
            transcendentals=0,
        ),
    )(info, *operands)
    return result


def make_on_device(n_row, n_col):
    def on_device(rhs_scen, factor_panels):
        rows_here = factor_panels.shape[0]
        lanes = NB // rows_here
        planes = n_col // lanes
        n_y = n_row // CORES
        members = lanes * n_y * CORES
        row, col = lax.axis_index("row"), lax.axis_index("col")
        y, core = row // CORES, row % CORES
        plane, lane = col // lanes, col % lanes
        my_block = (row * n_col + col) // lanes

        def device(y, core, plane, lane):
            return (y * CORES + core) * n_col + plane * lanes + lane

        def send(value, pairs):
            return lax.ppermute(value, AXES, pairs)

        def lane_gather(value, cores, zs):
            out = [value]
            for d in range(1, lanes):
                pairs = [
                    (device(t, c, z, (m + d) % lanes), device(t, c, z, m))
                    for t in range(n_y) for c in cores for z in zs for m in range(lanes)
                ]
                out.append(send(value, pairs))
            return out

        def y_gather(value, cores):
            out = [value]
            for d in range(1, n_y):
                pairs = [
                    (device((t + d) % n_y, c, z, m), device(t, c, z, m))
                    for t in range(n_y) for c in cores for z in range(planes) for m in range(lanes)
                ]
                out.append(send(value, pairs))
            return out

        def ahead(own, k):
            return [
                send(own, [(device(0, 0, k, (m + d) % lanes), device(0, 0, k + 1, m)) for m in range(lanes)])
                for d in range(lanes)
            ]

        lane_places = [(lane + d) % lanes for d in range(lanes)]

        def scatter_y(own, k):
            size = rows_here // n_y
            piece = own[:size]
            for t in range(1, n_y):
                cut = own[t * size : (t + 1) * size]
                got = send(cut, [(device(0, 0, k, m), device(t, 0, k, m)) for m in range(lanes)])
                piece = jnp.where(y == t, got, piece)
            return piece

        def plane_rounds(k):
            left = sorted((z for z in range(planes) if z != k), key=lambda z: -abs(z - k))
            half = max(planes // 2, 1)
            holders, rounds = [k], []
            while half:
                pairs = []
                for h in list(holders):
                    for z in (h ^ half, *left):
                        if z in left:
                            pairs.append((h, z))
                            holders.append(z)
                            left.remove(z)
                            break
                if pairs:
                    rounds.append(pairs)
                half //= 2
            while left:
                pairs = [(h, z) for h, z in zip(list(holders), list(left))]
                for _, z in pairs:
                    left.remove(z)
                    holders.append(z)
                rounds.append(pairs)
            return rounds

        def plane_send(piece, zpairs):
            got = send(
                piece,
                [
                    (device(t, 0, a, m), device(t, 0, b, m))
                    for a, b in zpairs for t in range(n_y) for m in range(lanes)
                ],
            )
            new = functools.reduce(jnp.logical_or, [plane == b for _, b in zpairs])
            return jnp.where(new, got, piece)

        def core_send(value):
            got = send(
                value,
                [
                    (device(t, 0, z, m), device(t, 1, z, m))
                    for t in range(n_y) for z in range(planes) for m in range(lanes)
                ],
            )
            return jnp.where(core == 0, value, got)

        tree_places = [
            ((lane + dm) % lanes) * n_y + (y + dy) % n_y for dy in range(n_y) for dm in range(lanes)
        ]

        extra = NB // members
        start_places = [
            (((lane + dm) % lanes) * n_y + (y + dy) % n_y) * CORES + (core + dc) % CORES
            for dc in range(CORES) for dy in range(n_y) for dm in range(lanes)
        ]
        first = rhs_scen[:, :NB].reshape(-1, lanes, n_y, CORES, extra).transpose(0, 2, 3, 1, 4)
        first = jnp.broadcast_to(
            first[:, :, :, None], (first.shape[0], n_y, CORES, planes, lanes, extra)
        ).reshape(first.shape[0], n_row * n_col, extra)
        outgoing = jnp.concatenate(
            [rhs_scen.reshape(rhs_scen.shape[0], n_row * n_col, rows_here), first], axis=2
        )
        regrouped = lax.all_to_all(outgoing, AXES, split_axis=1, concat_axis=0, tiled=True)
        regrouped = regrouped.reshape(-1, rows_here + extra)
        current = jnp.transpose(regrouped[:, :rows_here]).astype(jnp.float32)
        piece = jnp.transpose(regrouped[:, rows_here:])
        both = range(CORES)
        whole = jnp.concatenate(lane_gather(piece, both, range(planes)), axis=0)
        whole = jnp.concatenate(y_gather(whole, both), axis=0)
        other = send(
            whole,
            [
                (device(t, 1 - c, z, m), device(t, c, z, m))
                for t in range(n_y) for c in both for z in range(planes) for m in range(lanes)
            ],
        )
        halves = [whole, other]
        pieces = [h[i * extra : (i + 1) * extra] for h in halves for i in range(members // CORES)]

        def run(current, terms, types):
            return steps(current, factor_panels, terms, my_block, types)

        current, own1 = run(current, [(0, pieces, start_places)], [jnp.float32, jnp.bfloat16])

        def tree_start(own, k):
            piece = scatter_y(own, k)
            rounds = plane_rounds(k)
            return piece, rounds

        def tree_end(piece):
            got = jnp.concatenate(lane_gather(piece, [0], range(planes)), axis=0)
            return jnp.concatenate(y_gather(got, [0]), axis=0)

        hop1 = ahead(own1, 1)
        piece1, rounds1 = tree_start(own1, 1)
        fwd = send(hop1[0], [(device(0, 0, 2, m), device(0, 0, 3, m)) for m in range(lanes)])
        (own2,) = run(current, [(1, hop1, lane_places)], [jnp.bfloat16])
        hop2 = ahead(own2, 2)
        piece1 = after(piece1, own2)
        fwd_all = [fwd] + [
            send(fwd, [(device(0, 0, 3, (m + d) % lanes), device(0, 0, 3, m)) for m in range(lanes)])
            for d in range(1, lanes)
        ]
        (current_c,) = run(current, [(1, fwd_all, lane_places)], [jnp.float32])
        for pairs in rounds1:
            piece1 = plane_send(piece1, pairs)
        piece2, rounds2 = tree_start(own2, 2)
        (own3,) = run(current_c, [(2, hop2, lane_places)], [jnp.bfloat16])
        piece3, rounds3 = tree_start(own3, 3)
        piece1 = after(piece1, own3)
        piece2 = after(piece2, own3)
        got1 = tree_end(piece1)
        for pairs in rounds2:
            piece2 = plane_send(piece2, pairs)
        all1 = core_send(got1)
        for pairs in rounds3:
            piece3 = plane_send(piece3, pairs)
        got2 = tree_end(piece2)
        all2 = core_send(got2)
        (current,) = run(
            current,
            [(1, split(all1, tree_places), tree_places), (2, split(all2, tree_places), tree_places)],
            [jnp.float32],
        )
        got3 = tree_end(piece3)
        all3 = core_send(got3)
        (out,) = run(current, [(3, split(all3, tree_places), tree_places)], [jnp.float32])
        return out

    def split(whole, places):
        size = whole.shape[0] // len(places)
        return [whole[i * size : (i + 1) * size] for i in range(len(places))]

    return on_device


def solution(mesh):
    placed = (P(AXES, None), P(AXES, None))
    on_device = make_on_device(mesh.shape["row"], mesh.shape["col"])
    return jax.shard_map(
        on_device, mesh=mesh, in_specs=placed, out_specs=P(AXES, None), check_vma=False
    )
```

```python
import functools

import jax
import jax.numpy as jnp
from jax import lax
from jax.experimental import pallas as pl
from jax.experimental.pallas import tpu as pltpu
from jax.sharding import PartitionSpec as P

NB = 2048
STEPS = 4
AXES = ("row", "col")
CORES = 2
TILE = 256
KERNEL_VMEM = 50 * 1024 * 1024


def after(value, *others):
    return lax.optimization_barrier((value, *others))[0]


def step_kernel(plan, tile, *refs):
    terms, n_arrays, outs = plan
    info, current, panels = refs[:3]
    arrays = refs[3 : 3 + n_arrays]
    results = refs[3 + n_arrays : 3 + n_arrays + len(outs)]
    current_here, result_here, panels_here, held, sems, piece_sems, out_sems = refs[3 + n_arrays + len(outs) :]
    rows = current.shape[0]
    tiles = rows // tile
    n_terms = len(terms)

    copies, started = [], 0
    for t, (_, _, pieces) in enumerate(terms):
        for array, twin, first, size, place in pieces:
            start = pl.multiple_of(info[place] * size, size)

            def copy(source):
                return pltpu.make_async_copy(
                    arrays[source].at[pl.ds(first, size), :],
                    held.at[t, pl.ds(start, size), :],
                    piece_sems.at[started],
                )

            if twin is None:
                copy(array).start()
            else:
                pl.when(info[0] == 0)(lambda: copy(array).start())
                pl.when(info[0] != 0)(lambda: copy(twin).start())
            copies.append(copy(array))
            started += 1

    def panel_copy(t, i):
        k = terms[t][0]
        return pltpu.make_async_copy(
            panels.at[pl.ds(i * tile, tile), pl.ds(k * NB, NB)],
            panels_here.at[t, pl.ds(i * tile, tile), :],
            sems.at[t, i],
        )

    def current_copy(i):
        at = pl.ds(i * tile, tile)
        return pltpu.make_async_copy(current.at[at, :], current_here.at[at, :], sems.at[n_terms, i])

    for i in range(tiles):
        for t in range(n_terms):
            panel_copy(t, i).start()
        current_copy(i).start()
    for copy in copies:
        copy.wait()
    sent = []
    for i in range(tiles):
        at = pl.ds(i * tile, tile)
        current_copy(i).wait()
        value = current_here[at, :]
        for t in range(n_terms):
            panel_copy(t, i).wait()
            product = jnp.dot(panels_here[t, at, :], held[t], preferred_element_type=jnp.float32)
            value = jnp.where(info[terms[t][1]] == 1, product, value - product)
        for o, (dtype, first, size, far) in enumerate(outs):
            low, high = max(first, i * tile), min(first + size, (i + 1) * tile)
            if low < high:
                part = value[low - i * tile : high - i * tile].astype(dtype)
                if far:
                    result_here[at, :] = part
                    out = pltpu.make_async_copy(result_here.at[at, :], results[o].at[at, :], out_sems.at[i])
                    out.start()
                    sent.append(out)
                else:
                    results[o][pl.ds(low - first, high - low), :] = part
    for out in sent:
        out.wait()


def steps(current, factor_panels, terms, my_block, core, outs):
    rows, scenarios = current.shape
    tile = min(TILE, rows)
    info, arrays, plan = [core], [], []

    def index(array):
        if array is None:
            return None
        for i, other in enumerate(arrays):
            if other is array:
                return i
        arrays.append(array)
        return len(arrays) - 1

    for k, pieces in terms:
        info.append(my_block == k)
        flag, listed = len(info) - 1, []
        for array, twin, first, size, place in pieces:
            info.append(place)
            listed.append((index(array), index(twin), first, size, len(info) - 1))
        plan.append((k, flag, tuple(listed)))
    info = jnp.stack([jnp.asarray(x, jnp.int32) for x in info])
    n_terms = len(terms)
    n_pieces = sum(len(pieces) for _, pieces in terms)
    far = any(out[3] for out in outs)
    anywhere = pl.BlockSpec(memory_space=pl.ANY)
    return pl.pallas_call(
        functools.partial(step_kernel, (tuple(plan), len(arrays), tuple(outs)), tile),
        in_specs=[pl.BlockSpec(memory_space=pltpu.SMEM), anywhere, pl.BlockSpec(memory_space=pltpu.HBM)]
        + [anywhere] * len(arrays),
        out_specs=[pl.BlockSpec(memory_space=pltpu.HBM if out[3] else pltpu.VMEM) for out in outs],
        out_shape=[jax.ShapeDtypeStruct((size, scenarios), dtype) for dtype, _, size, _ in outs],
        scratch_shapes=[
            pltpu.VMEM((rows, scenarios), jnp.float32),
            pltpu.VMEM((rows if far else 8, scenarios), jnp.float32),
            pltpu.VMEM((n_terms, rows, NB), jnp.bfloat16),
            pltpu.VMEM((n_terms, NB, scenarios), jnp.bfloat16),
            pltpu.SemaphoreType.DMA((n_terms + 1, rows // tile)),
            pltpu.SemaphoreType.DMA((n_pieces,)),
            pltpu.SemaphoreType.DMA((rows // tile,)),
        ],
        compiler_params=pltpu.CompilerParams(vmem_limit_bytes=KERNEL_VMEM),
        cost_estimate=pl.CostEstimate(
            flops=2 * rows * NB * scenarios * n_terms,
            bytes_accessed=2 * rows * NB * n_terms + 8 * rows * scenarios,
            transcendentals=0,
        ),
    )(info, current, factor_panels, *arrays)


def make_on_device(n_row, n_col):
    def on_device(rhs_scen, factor_panels):
        rows_here = factor_panels.shape[0]
        lanes = NB // rows_here
        planes = n_col // lanes
        n_y = n_row // CORES
        members = lanes * n_y * CORES
        row, col = lax.axis_index("row"), lax.axis_index("col")
        y, core = row // CORES, row % CORES
        plane, lane = col // lanes, col % lanes
        my_block = (row * n_col + col) // lanes

        def device(y, core, plane, lane):
            return (y * CORES + core) * n_col + plane * lanes + lane

        def send(value, pairs):
            return lax.ppermute(value, AXES, pairs)

        def lane_gather(value, cores, zs, ys=range(n_y)):
            out = [value]
            for d in range(1, lanes):
                pairs = [
                    (device(t, c, z, (m + d) % lanes), device(t, c, z, m))
                    for t in ys for c in cores for z in zs for m in range(lanes)
                ]
                out.append(send(value, pairs))
            return out

        def y_gather(value, cores):
            out = [value]
            for d in range(1, n_y):
                pairs = [
                    (device((t + d) % n_y, c, z, m), device(t, c, z, m))
                    for t in range(n_y) for c in cores for z in range(planes) for m in range(lanes)
                ]
                out.append(send(value, pairs))
            return out

        def ahead(own, k):
            return [
                send(own, [(device(0, 0, k, (m + d) % lanes), device(0, 0, k + 1, m)) for m in range(lanes)])
                for d in range(lanes)
            ]

        lane_places = [(lane + d) % lanes for d in range(lanes)]

        def scatter_y(cuts, sources):
            piece = cuts[0]
            for t in range(1, n_y):
                pairs = [(device(0, 0, k, m), device(t, 0, k, m)) for k in sources for m in range(lanes)]
                piece = jnp.where(y == t, send(cuts[t], pairs), piece)
            return piece

        def along_planes(piece, sources):
            got = []
            for d in range(1, planes):
                pairs = [
                    (device(t, 0, k, m), device(t, 0, (k + d) % planes, m))
                    for k in sources for t in range(n_y) for m in range(lanes)
                ]
                got.append(send(piece, pairs))
            out = []
            for k in sources:
                value = piece
                for d in range(1, planes):
                    value = jnp.where(plane == (k + d) % planes, got[d - 1], value)
                out.append(value)
            return out

        def core_send(value):
            return send(
                value,
                [
                    (device(t, 0, z, m), device(t, 1, z, m))
                    for t in range(n_y) for z in range(planes) for m in range(lanes)
                ],
            )

        tree_places = [
            ((lane + dm) % lanes) * n_y + (y + dy) % n_y for dy in range(n_y) for dm in range(lanes)
        ]

        extra = NB // members
        start_places = [
            (((lane + dm) % lanes) * n_y + (y + dy) % n_y) * CORES + (core + dc) % CORES
            for dc in range(CORES) for dy in range(n_y) for dm in range(lanes)
        ]
        first = rhs_scen[:, :NB].reshape(-1, lanes, n_y, CORES, extra).transpose(0, 2, 3, 1, 4)
        first = jnp.broadcast_to(
            first[:, :, :, None], (first.shape[0], n_y, CORES, planes, lanes, extra)
        ).reshape(first.shape[0], n_row * n_col, extra)
        outgoing = jnp.concatenate(
            [rhs_scen.reshape(rhs_scen.shape[0], n_row * n_col, rows_here), first], axis=2
        )
        regrouped = lax.all_to_all(outgoing, AXES, split_axis=1, concat_axis=0, tiled=True)
        regrouped = regrouped.reshape(-1, rows_here + extra)
        current = jnp.transpose(regrouped[:, :rows_here]).astype(jnp.float32)
        piece = jnp.transpose(regrouped[:, rows_here:])
        both = range(CORES)
        whole = jnp.concatenate(lane_gather(piece, both, range(planes)), axis=0)
        whole = jnp.concatenate(y_gather(whole, both), axis=0)
        other = send(
            whole,
            [
                (device(t, 1 - c, z, m), device(t, c, z, m))
                for t in range(n_y) for c in both for z in range(planes) for m in range(lanes)
            ],
        )
        per_core = members // CORES
        pieces = [
            (half, None, i * extra, extra, start_places[c * per_core + i])
            for c, half in enumerate([whole, other]) for i in range(per_core)
        ]

        def run(current, terms, outs):
            return steps(current, factor_panels, terms, my_block, core, outs)

        cut = rows_here // n_y
        f32_rows = (jnp.float32, 0, rows_here, False)
        own_rows = (jnp.bfloat16, 0, rows_here, False)
        own_cuts = [(jnp.bfloat16, t * cut, cut, False) for t in range(n_y)]

        def lane_pieces(parts):
            return [(part, None, 0, rows_here, lane_places[d]) for d, part in enumerate(parts)]

        def gather_plane(value):
            mine = jnp.concatenate(lane_gather(value, [0], range(planes)), axis=0)
            far = y_gather(mine, [0])
            return [(part, core_send(part)) for part in far]

        def tree_pieces(arrays, first, size, stride):
            return [
                (mine, other, m * stride + first, size, tree_places[i * lanes + m])
                for i, (mine, other) in enumerate(arrays) for m in range(lanes)
            ]

        current, own1, *cuts1 = run(current, [(0, pieces)], [f32_rows, own_rows, *own_cuts])

        hop1 = ahead(own1, 1)
        near = jnp.where(plane == 2, after(hop1[0], *hop1[1:]), own1)
        pairs = [(device(0, 0, a, m), device(0, 0, b, m)) for a, b in ((2, 3), (1, 0)) for m in range(lanes)]
        passed = send(near, pairs)
        own2, *cuts2 = run(current, [(1, lane_pieces(hop1))], [own_rows, *own_cuts])
        passed = after(passed, own2)
        near = jnp.where((plane == 1) | (plane == 2), near, passed)
        hop2 = ahead(own2, 2)
        served = STEPS
        while served < planes:
            pairs = [
                (device(0, 0, z, m), device(0, 0, z + served, m))
                for z in range(min(served, planes - served)) for m in range(lanes)
            ]
            near = jnp.where((plane >= served) & (plane < 2 * served), send(near, pairs), near)
            served *= 2
        across = lane_gather(near, [0], [z for z in range(planes) if z != 2], [0])
        (chained,) = run(current, [(1, lane_pieces([passed, *across[1:]]))], [f32_rows])
        cuts3 = run(chained, [(2, lane_pieces(hop2))], own_cuts)

        near1 = after(near, own2)
        low1 = [near1] + [jnp.where(plane == 2, a, b) for a, b in zip(hop1[1:], across[1:])]
        for t in range(1, n_y):
            pairs = [(device(0, 0, z, m), device(t, 0, z, m)) for z in range(planes) for m in range(lanes)]
            near1 = jnp.where(y == t, send(near1, pairs), near1)
        high1 = lane_gather(near1, [0], range(planes), range(1, n_y))
        all1 = jnp.concatenate([jnp.where(y == 0, a, b) for a, b in zip(low1, high1)], axis=0)
        other1 = core_send(all1)

        cuts23 = [jnp.where(plane == 2, a, b) for a, b in zip(cuts2, cuts3)]
        piece23 = scatter_y(cuts23, [2, 3])
        piece23 = jnp.concatenate(along_planes(piece23, [2, 3]), axis=0)
        all23 = gather_plane(piece23)
        pieces1 = [(all1, other1, d * rows_here, rows_here, lane_places[d]) for d in range(lanes)]
        (current,) = run(current, [(1, pieces1)], [f32_rows])
        (out,) = run(
            current,
            [(2, tree_pieces(all23, 0, cut, 2 * cut)), (3, tree_pieces(all23, cut, cut, 2 * cut))],
            [(jnp.float32, 0, rows_here, True)],
        )
        return out

    return on_device


def solution(mesh):
    placed = (P(AXES, None), P(AXES, None))
    on_device = make_on_device(mesh.shape["row"], mesh.shape["col"])
    return jax.shard_map(
        on_device, mesh=mesh, in_specs=placed, out_specs=P(AXES, None), check_vma=False
    )
```

```python
import functools

import jax
import jax.numpy as jnp
from jax import lax
from jax.experimental import pallas as pl
from jax.experimental.pallas import tpu as pltpu
from jax.sharding import PartitionSpec as P

NB = 2048
STEPS = 4
AXES = ("row", "col")
CORES = 2
TILE = 256
DEPTH = 512
KERNEL_VMEM = 40 * 1024 * 1024


def after(value, *others):
    return lax.optimization_barrier((value, *others))[0]


def step_kernel(terms, n_arrays, outs, where_am_i, *refs):
    current, panels = refs[:2]
    arrays = refs[2 : 2 + n_arrays]
    results = refs[2 + n_arrays : 2 + n_arrays + len(outs)]
    current_here, totals, panels_here, held, sems, piece_sems, current_sem, out_sems = refs[2 + n_arrays + len(outs) :]
    rows = current.shape[0]
    depth = min(DEPTH, NB)
    chunks = NB // depth
    here = where_am_i()

    copies = []
    for t, (_, pieces) in enumerate(terms):
        for array, twin, first, size, place in pieces:
            start = pl.multiple_of(place(here) * size, size)

            def copy(source):
                return pltpu.make_async_copy(
                    arrays[source].at[pl.ds(first, size), :],
                    held.at[t, pl.ds(start, size), :],
                    piece_sems.at[len(copies)],
                )

            if twin is None:
                copy(array).start()
            else:
                pl.when(here.core == 0)(lambda: copy(array).start())
                pl.when(here.core != 0)(lambda: copy(twin).start())
            copies.append(copy(array))

    def panel_copy(t, i):
        k = terms[t][0]
        return pltpu.make_async_copy(
            panels.at[:, pl.ds(k * NB + i * depth, depth)], panels_here.at[t, i], sems.at[t, i]
        )

    for t in range(len(terms)):
        for i in range(chunks):
            panel_copy(t, i).start()
    current_copy = pltpu.make_async_copy(current, current_here, current_sem)
    current_copy.start()
    for copy in copies:
        copy.wait()
    for t in range(len(terms)):
        for i in range(chunks):
            panel_copy(t, i).wait()
            part = jnp.dot(
                panels_here[t, i], held[t, pl.ds(i * depth, depth), :], preferred_element_type=jnp.float32
            )
            totals[t] = part if i == 0 else totals[t] + part
    current_copy.wait()
    sent = []
    tile = min(TILE, rows)
    for i in range(rows // tile):
        at = pl.ds(i * tile, tile)
        value = current_here[at, :]
        for t, (k, _) in enumerate(terms):
            product = totals[t, at, :]
            value = jnp.where(here.block == k, product, value - product)
        for o, (dtype, first, size, far) in enumerate(outs):
            low, high = max(first, i * tile), min(first + size, (i + 1) * tile)
            if low < high:
                part = value[low - i * tile : high - i * tile].astype(dtype)
                if far:
                    current_here[at, :] = part
                    out = pltpu.make_async_copy(current_here.at[at, :], results[o].at[at, :], out_sems.at[i])
                    out.start()
                    sent.append(out)
                else:
                    results[o][pl.ds(low - first, high - low), :] = part
    for out in sent:
        out.wait()


def steps(current, factor_panels, terms, outs, where_am_i):
    rows, scenarios = current.shape
    arrays, plan = [], []

    def index(array):
        if array is None:
            return None
        for i, other in enumerate(arrays):
            if other is array:
                return i
        arrays.append(array)
        return len(arrays) - 1

    for k, pieces in terms:
        plan.append((k, tuple((index(a), index(b), first, size, place) for a, b, first, size, place in pieces)))
    n_terms = len(terms)
    depth = min(DEPTH, NB)
    n_pieces = sum(len(pieces) for _, pieces in terms)
    anywhere = pl.BlockSpec(memory_space=pl.ANY)
    return pl.pallas_call(
        functools.partial(step_kernel, tuple(plan), len(arrays), tuple(outs), where_am_i),
        in_specs=[anywhere] * (2 + len(arrays)),
        out_specs=[anywhere if out[3] else pl.BlockSpec(memory_space=pltpu.VMEM) for out in outs],
        out_shape=[jax.ShapeDtypeStruct((size, scenarios), dtype) for dtype, _, size, _ in outs],
        scratch_shapes=[
            pltpu.VMEM((rows, scenarios), jnp.float32),
            pltpu.VMEM((n_terms, rows, scenarios), jnp.float32),
            pltpu.VMEM((n_terms, NB // depth, rows, depth), jnp.bfloat16),
            pltpu.VMEM((n_terms, NB, scenarios), jnp.bfloat16),
            pltpu.SemaphoreType.DMA((n_terms, NB // depth)),
            pltpu.SemaphoreType.DMA((n_pieces,)),
            pltpu.SemaphoreType.DMA,
            pltpu.SemaphoreType.DMA((rows // min(TILE, rows),)),
        ],
        compiler_params=pltpu.CompilerParams(vmem_limit_bytes=KERNEL_VMEM),
        cost_estimate=pl.CostEstimate(
            flops=2 * rows * NB * scenarios * n_terms,
            bytes_accessed=8 * rows * scenarios,
            transcendentals=0,
        ),
    )(current, factor_panels, *arrays)


class Place:
    def __init__(self, n_col, lanes):
        row, col = lax.axis_index("row"), lax.axis_index("col")
        self.y, self.core = row // CORES, row % CORES
        self.plane, self.lane = col // lanes, col % lanes
        self.block = (row * n_col + col) // lanes


def make_on_device(n_row, n_col):
    def on_device(rhs_scen, factor_panels):
        rows_here = factor_panels.shape[0]
        lanes = NB // rows_here
        planes = n_col // lanes
        n_y = n_row // CORES
        members = lanes * n_y * CORES
        where_am_i = functools.partial(Place, n_col, lanes)
        here = where_am_i()
        y, core, plane = here.y, here.core, here.plane

        def device(y, core, plane, lane):
            return (y * CORES + core) * n_col + plane * lanes + lane

        def send(value, pairs):
            return lax.ppermute(value, AXES, pairs)

        def lane_gather(value, cores, zs, ys=range(n_y)):
            out = [value]
            for d in range(1, lanes):
                pairs = [
                    (device(t, c, z, (m + d) % lanes), device(t, c, z, m))
                    for t in ys for c in cores for z in zs for m in range(lanes)
                ]
                out.append(send(value, pairs))
            return out

        def y_gather(value, cores):
            out = [value]
            for d in range(1, n_y):
                pairs = [
                    (device((t + d) % n_y, c, z, m), device(t, c, z, m))
                    for t in range(n_y) for c in cores for z in range(planes) for m in range(lanes)
                ]
                out.append(send(value, pairs))
            return out

        def ahead(own, k):
            return [
                send(own, [(device(0, 0, k, (m + d) % lanes), device(0, 0, k + 1, m)) for m in range(lanes)])
                for d in range(lanes)
            ]

        lane_places = [functools.partial(lambda d, at: (at.lane + d) % lanes, d) for d in range(lanes)]

        def scatter_y(cuts, sources):
            piece = cuts[0]
            for t in range(1, n_y):
                pairs = [(device(0, 0, k, m), device(t, 0, k, m)) for k in sources for m in range(lanes)]
                piece = jnp.where(y == t, send(cuts[t], pairs), piece)
            return piece

        def along_planes(piece, sources):
            got = []
            for d in range(1, planes):
                pairs = [
                    (device(t, 0, k, m), device(t, 0, (k + d) % planes, m))
                    for k in sources for t in range(n_y) for m in range(lanes)
                ]
                got.append(send(piece, pairs))
            out = []
            for k in sources:
                value = piece
                for d in range(1, planes):
                    value = jnp.where(plane == (k + d) % planes, got[d - 1], value)
                out.append(value)
            return out

        def core_send(value):
            return send(
                value,
                [
                    (device(t, 0, z, m), device(t, 1, z, m))
                    for t in range(n_y) for z in range(planes) for m in range(lanes)
                ],
            )

        tree_places = [
            functools.partial(lambda dy, dm, at: ((at.lane + dm) % lanes) * n_y + (at.y + dy) % n_y, dy, dm)
            for dy in range(n_y) for dm in range(lanes)
        ]

        extra = NB // members
        start_places = [
            functools.partial(lambda dc, q, at: q(at) * CORES + (at.core + dc) % CORES, dc, q)
            for dc in range(CORES) for q in tree_places
        ]
        first = rhs_scen[:, :NB].reshape(-1, lanes, n_y, CORES, extra).transpose(0, 2, 3, 1, 4)
        first = jnp.broadcast_to(
            first[:, :, :, None], (first.shape[0], n_y, CORES, planes, lanes, extra)
        ).reshape(first.shape[0], n_row * n_col, extra)
        outgoing = jnp.concatenate(
            [rhs_scen.reshape(rhs_scen.shape[0], n_row * n_col, rows_here), first], axis=2
        )
        regrouped = lax.all_to_all(outgoing, AXES, split_axis=1, concat_axis=0, tiled=True)
        regrouped = regrouped.reshape(-1, rows_here + extra)
        current = jnp.transpose(regrouped[:, :rows_here]).astype(jnp.float32)
        piece = jnp.transpose(regrouped[:, rows_here:])
        both = range(CORES)
        whole = jnp.concatenate(lane_gather(piece, both, range(planes)), axis=0)
        whole = jnp.concatenate(y_gather(whole, both), axis=0)
        other = send(
            whole,
            [
                (device(t, 1 - c, z, m), device(t, c, z, m))
                for t in range(n_y) for c in both for z in range(planes) for m in range(lanes)
            ],
        )
        per_core = members // CORES
        pieces = [
            (half, None, i * extra, extra, start_places[c * per_core + i])
            for c, half in enumerate([whole, other]) for i in range(per_core)
        ]

        def run(current, terms, outs):
            return steps(current, factor_panels, terms, outs, where_am_i)

        cut = rows_here // n_y
        f32_rows = (jnp.float32, 0, rows_here, False)
        own_rows = (jnp.bfloat16, 0, rows_here, False)
        own_cuts = [(jnp.bfloat16, t * cut, cut, False) for t in range(n_y)]

        def lane_pieces(parts):
            return [(part, None, 0, rows_here, lane_places[d]) for d, part in enumerate(parts)]

        def gather_plane(value):
            mine = jnp.concatenate(lane_gather(value, [0], range(planes)), axis=0)
            far = y_gather(mine, [0])
            return [(part, core_send(part)) for part in far]

        def tree_pieces(arrays, first, size, stride):
            return [
                (mine, other, m * stride + first, size, tree_places[i * lanes + m])
                for i, (mine, other) in enumerate(arrays) for m in range(lanes)
            ]

        def to_rows(parts, order):
            whole = jnp.concatenate(parts, axis=0)
            kept = jnp.where((y == 0) & (core == 0), whole, 0).astype(whole.dtype)
            return kept, lax.psum(kept, "row", axis_index_groups=[order])

        current, own1 = run(current, [(0, pieces)], [f32_rows, own_rows])

        hop1 = ahead(own1, 1)
        near = jnp.where(plane == 2, after(hop1[0], *hop1[1:]), own1)
        pairs = [(device(0, 0, a, m), device(0, 0, b, m)) for a, b in ((2, 3), (1, 0)) for m in range(lanes)]
        passed = send(near, pairs)
        (own2,) = run(current, [(1, lane_pieces(hop1))], [own_rows])
        passed = after(passed, own2)
        near = jnp.where((plane == 1) | (plane == 2), near, passed)
        hop2 = ahead(own2, 2)
        served = STEPS
        while served < planes:
            pairs = [
                (device(0, 0, z, m), device(0, 0, z + served, m))
                for z in range(min(served, planes - served)) for m in range(lanes)
            ]
            near = jnp.where((plane >= served) & (plane < 2 * served), send(near, pairs), near)
            served *= 2
        across = lane_gather(near, [0], [z for z in range(planes) if z != 2], [0])
        (chained,) = run(current, [(1, lane_pieces([passed, *across[1:]]))], [f32_rows])

        start2 = after(own2, *across[1:])
        near2 = start2
        for d in range(1, planes):
            if d != 1:
                pairs = [(device(0, 0, 2, m), device(0, 0, (2 + d) % planes, m)) for m in range(lanes)]
                near2 = jnp.where(plane == (2 + d) % planes, send(start2, pairs), near2)
        order = list(range(n_row))
        parts1 = [near] + [jnp.where(plane == 2, a, b) for a, b in zip(hop1[1:], across[1:])]
        kept1, whole1 = to_rows(parts1, order)
        chained = after(chained, kept1, near2)
        cuts3 = run(chained, [(2, lane_pieces(hop2))], own_cuts)
        across2 = lane_gather(near2, [0], [z for z in range(planes) if z != 3], [0])
        near2 = jnp.where(plane == 3, hop2[0], near2)
        parts2 = [near2] + [jnp.where(plane == 3, a, b) for a, b in zip(hop2[1:], across2[1:])]
        kept2, whole2 = to_rows(parts2, order[::-1])

        (piece3,) = along_planes(scatter_y(cuts3, [3]), [3])
        piece3 = after(piece3, kept2)
        all3 = gather_plane(piece3)

        def whole_pieces(whole):
            return [(whole, None, d * rows_here, rows_here, lane_places[d]) for d in range(lanes)]

        (current,) = run(current, [(1, whole_pieces(whole1)), (2, whole_pieces(whole2))], [f32_rows])
        (out,) = run(current, [(3, tree_pieces(all3, 0, cut, cut))], [(jnp.float32, 0, rows_here, True)])
        return out

    return on_device


def solution(mesh):
    placed = (P(AXES, None), P(AXES, None))
    on_device = make_on_device(mesh.shape["row"], mesh.shape["col"])
    return jax.shard_map(
        on_device, mesh=mesh, in_specs=placed, out_specs=P(AXES, None), check_vma=False
    )
```

```python
import functools

import jax
import jax.numpy as jnp
from jax import lax
from jax.experimental import pallas as pl
from jax.experimental.pallas import tpu as pltpu
from jax.sharding import PartitionSpec as P

NB = 2048
STEPS = 4
AXES = ("row", "col")
CORES = 2
TILE = 256
DEPTH = 512
KERNEL_VMEM = 40 * 1024 * 1024


def after(value, *others):
    return lax.optimization_barrier((value, *others))[0]


def step_kernel(terms, n_arrays, outs, where_am_i, active, *refs):
    current, panels = refs[:2]
    arrays = refs[2 : 2 + n_arrays]
    results = refs[2 + n_arrays : 2 + n_arrays + len(outs)]
    current_here, totals, panels_here, held, sems, piece_sems, current_sem, out_sems = refs[2 + n_arrays + len(outs) :]
    rows = current.shape[0]
    depth = min(DEPTH, NB)
    chunks = NB // depth
    here = where_am_i()

    def work():
        copies = []
        for t, (_, pieces) in enumerate(terms):
            for array, twin, first, size, place in pieces:
                start = pl.multiple_of(place(here) * size, size)

                def copy(source):
                    return pltpu.make_async_copy(
                        arrays[source].at[pl.ds(first, size), :],
                        held.at[t, pl.ds(start, size), :],
                        piece_sems.at[len(copies)],
                    )

                if twin is None:
                    copy(array).start()
                else:
                    pl.when(here.core == 0)(lambda: copy(array).start())
                    pl.when(here.core != 0)(lambda: copy(twin).start())
                copies.append(copy(array))

        def panel_copy(t, i):
            k = terms[t][0]
            return pltpu.make_async_copy(
                panels.at[:, pl.ds(k * NB + i * depth, depth)], panels_here.at[t, i], sems.at[t, i]
            )

        for t in range(len(terms)):
            for i in range(chunks):
                panel_copy(t, i).start()
        current_copy = pltpu.make_async_copy(current, current_here, current_sem)
        current_copy.start()
        for copy in copies:
            copy.wait()
        for t in range(len(terms)):
            for i in range(chunks):
                panel_copy(t, i).wait()
                part = jnp.dot(
                    panels_here[t, i], held[t, pl.ds(i * depth, depth), :], preferred_element_type=jnp.float32
                )
                totals[t] = part if i == 0 else totals[t] + part
        current_copy.wait()
        sent = []
        tile = min(TILE, rows)
        for i in range(rows // tile):
            at = pl.ds(i * tile, tile)
            value = current_here[at, :]
            for t, (k, _) in enumerate(terms):
                product = totals[t, at, :]
                value = jnp.where(here.block == k, product, value - product)
            for o, (dtype, first, size, far) in enumerate(outs):
                low, high = max(first, i * tile), min(first + size, (i + 1) * tile)
                if low < high:
                    part = value[low - i * tile : high - i * tile].astype(dtype)
                    if far:
                        current_here[at, :] = part
                        out = pltpu.make_async_copy(current_here.at[at, :], results[o].at[at, :], out_sems.at[i])
                        out.start()
                        sent.append(out)
                    else:
                        results[o][pl.ds(low - first, high - low), :] = part
        for out in sent:
            out.wait()

    if active is None:
        work()
    else:
        pl.when(active(here))(work)


def steps(current, factor_panels, terms, outs, where_am_i, active):
    rows, scenarios = current.shape
    arrays, plan = [], []

    def index(array):
        if array is None:
            return None
        for i, other in enumerate(arrays):
            if other is array:
                return i
        arrays.append(array)
        return len(arrays) - 1

    for k, pieces in terms:
        plan.append((k, tuple((index(a), index(b), first, size, place) for a, b, first, size, place in pieces)))
    n_terms = len(terms)
    depth = min(DEPTH, NB)
    n_pieces = sum(len(pieces) for _, pieces in terms)
    anywhere = pl.BlockSpec(memory_space=pl.ANY)
    return pl.pallas_call(
        functools.partial(step_kernel, tuple(plan), len(arrays), tuple(outs), where_am_i, active),
        in_specs=[anywhere] * (2 + len(arrays)),
        out_specs=[anywhere if out[3] else pl.BlockSpec(memory_space=pltpu.VMEM) for out in outs],
        out_shape=[jax.ShapeDtypeStruct((size, scenarios), dtype) for dtype, _, size, _ in outs],
        scratch_shapes=[
            pltpu.VMEM((rows, scenarios), jnp.float32),
            pltpu.VMEM((n_terms, rows, scenarios), jnp.float32),
            pltpu.VMEM((n_terms, NB // depth, rows, depth), jnp.bfloat16),
            pltpu.VMEM((n_terms, NB, scenarios), jnp.bfloat16),
            pltpu.SemaphoreType.DMA((n_terms, NB // depth)),
            pltpu.SemaphoreType.DMA((n_pieces,)),
            pltpu.SemaphoreType.DMA,
            pltpu.SemaphoreType.DMA((rows // min(TILE, rows),)),
        ],
        compiler_params=pltpu.CompilerParams(vmem_limit_bytes=KERNEL_VMEM),
        cost_estimate=pl.CostEstimate(
            flops=2 * rows * NB * scenarios * n_terms,
            bytes_accessed=8 * rows * scenarios,
            transcendentals=0,
        ),
    )(current, factor_panels, *arrays)


class Place:
    def __init__(self, n_col, lanes):
        row, col = lax.axis_index("row"), lax.axis_index("col")
        self.y, self.core = row // CORES, row % CORES
        self.plane, self.lane = col // lanes, col % lanes
        self.block = (row * n_col + col) // lanes


def make_on_device(n_row, n_col):
    def on_device(rhs_scen, factor_panels):
        rows_here = factor_panels.shape[0]
        lanes = NB // rows_here
        planes = n_col // lanes
        n_y = n_row // CORES
        members = lanes * n_y * CORES
        where_am_i = functools.partial(Place, n_col, lanes)
        here = where_am_i()
        y, core, plane = here.y, here.core, here.plane

        def device(y, core, plane, lane):
            return (y * CORES + core) * n_col + plane * lanes + lane

        def send(value, pairs):
            return lax.ppermute(value, AXES, pairs)

        def lane_gather(value, cores, zs, ys=range(n_y)):
            out = [value]
            for d in range(1, lanes):
                pairs = [
                    (device(t, c, z, (m + d) % lanes), device(t, c, z, m))
                    for t in ys for c in cores for z in zs for m in range(lanes)
                ]
                out.append(send(value, pairs))
            return out

        def y_gather(value, cores):
            out = [value]
            for d in range(1, n_y):
                pairs = [
                    (device((t + d) % n_y, c, z, m), device(t, c, z, m))
                    for t in range(n_y) for c in cores for z in range(planes) for m in range(lanes)
                ]
                out.append(send(value, pairs))
            return out

        def plane_gather(value, cores):
            first = lane_gather(value, cores, range(planes))
            far = y_gather(value, cores)[1:]
            return first + [part for got in far for part in lane_gather(got, cores, range(planes))]

        def ahead(own, k):
            return [
                send(own, [(device(0, 0, k, (m + d) % lanes), device(0, 0, k + 1, m)) for m in range(lanes)])
                for d in range(lanes)
            ]

        lane_places = [functools.partial(lambda d, at: (at.lane + d) % lanes, d) for d in range(lanes)]

        def scatter_y(cuts, sources):
            piece = cuts[0]
            for t in range(1, n_y):
                pairs = [(device(0, 0, k, m), device(t, 0, k, m)) for k in sources for m in range(lanes)]
                piece = jnp.where(y == t, send(cuts[t], pairs), piece)
            return piece

        def along_planes(piece, sources):
            got = []
            for d in range(1, planes):
                pairs = [
                    (device(t, 0, k, m), device(t, 0, (k + d) % planes, m))
                    for k in sources for t in range(n_y) for m in range(lanes)
                ]
                got.append(send(piece, pairs))
            out = []
            for k in sources:
                value = piece
                for d in range(1, planes):
                    value = jnp.where(plane == (k + d) % planes, got[d - 1], value)
                out.append(value)
            return out

        def core_send(value):
            return send(
                value,
                [
                    (device(t, 0, z, m), device(t, 1, z, m))
                    for t in range(n_y) for z in range(planes) for m in range(lanes)
                ],
            )

        tree_places = [
            functools.partial(lambda dy, dm, at: ((at.lane + dm) % lanes) * n_y + (at.y + dy) % n_y, dy, dm)
            for dy in range(n_y) for dm in range(lanes)
        ]

        extra = NB // members
        start_places = [
            functools.partial(lambda dc, q, at: q(at) * CORES + (at.core + dc) % CORES, dc, q)
            for dc in range(CORES) for q in tree_places
        ]
        first = rhs_scen[:, :NB].reshape(-1, lanes, n_y, CORES, extra).transpose(0, 2, 3, 1, 4)
        first = jnp.broadcast_to(
            first[:, :, :, None], (first.shape[0], n_y, CORES, planes, lanes, extra)
        ).reshape(first.shape[0], n_row * n_col, extra)
        outgoing = jnp.concatenate(
            [rhs_scen.reshape(rhs_scen.shape[0], n_row * n_col, rows_here), first], axis=2
        )
        regrouped = lax.all_to_all(outgoing, AXES, split_axis=1, concat_axis=0, tiled=True)
        regrouped = regrouped.reshape(-1, rows_here + extra)
        current = jnp.transpose(regrouped[:, :rows_here]).astype(jnp.float32)
        piece = jnp.transpose(regrouped[:, rows_here:])
        both = range(CORES)
        whole = jnp.concatenate(plane_gather(piece, both), axis=0)
        other = send(
            whole,
            [
                (device(t, 1 - c, z, m), device(t, c, z, m))
                for t in range(n_y) for c in both for z in range(planes) for m in range(lanes)
            ],
        )
        per_core = members // CORES
        pieces = [
            (half, None, i * extra, extra, start_places[c * per_core + i])
            for c, half in enumerate([whole, other]) for i in range(per_core)
        ]

        def run(current, terms, outs, only=None):
            active = None if only is None else lambda at: at.block == only
            return steps(current, factor_panels, terms, outs, where_am_i, active)

        cut = rows_here // n_y
        f32_rows = (jnp.float32, 0, rows_here, False)
        own_rows = (jnp.bfloat16, 0, rows_here, False)
        own_cuts = [(jnp.bfloat16, t * cut, cut, False) for t in range(n_y)]

        def lane_pieces(parts):
            return [(part, None, 0, rows_here, lane_places[d]) for d, part in enumerate(parts)]

        current, own1 = run(current, [(0, pieces)], [f32_rows, own_rows])

        def to_y(own, k):
            value = own
            for t in range(1, n_y):
                pairs = [(device(0, 0, k, m), device(t, 0, k, m)) for m in range(lanes)]
                value = jnp.where(y == t, send(own, pairs), value)
            return value

        def pairs_to(k, z, ys):
            return [(device(t, 0, k, m), device(t, 0, z, m)) for t in ys for m in range(lanes)]

        every_y = range(n_y)

        hop1 = ahead(own1, 1)
        near1 = after(to_y(own1, 1), hop1[0])
        crossed = [
            send(
                near1,
                [(device(0, 0, 1, (m + d) % lanes), device(0, 0, 3, m)) for m in range(lanes)]
                + (pairs_to(1, 2, every_y[1:]) if d == 1 else []),
            )
            for d in range(1, lanes)
        ]
        got1 = {z: send(near1, pairs_to(1, z, every_y)) for z in range(planes) if z not in (1, 2)}
        got1[2] = jnp.where(y == 0, hop1[0], crossed[0])
        (own2,) = run(current, [(1, lane_pieces(hop1))], [own_rows], 2)
        hop2 = ahead(own2, 2)
        (chained,) = run(current, [(1, lane_pieces([got1[3], *crossed]))], [f32_rows], 3)
        cuts3 = run(chained, [(2, lane_pieces(hop2))], own_cuts, 3)
        start2 = after(own2, chained)
        got2 = {z: send(start2, pairs_to(2, z, [0])) for z in range(planes) if z not in (2, 3)}
        got2[3] = hop2[0]

        piece3 = scatter_y(cuts3, [3])
        halves = []
        for value, got in ((near1, got1), (own2, got2)):
            for z, part in got.items():
                value = jnp.where(plane == z, part, value)
            halves.append(value)
        near2 = after(halves[1], cuts3[0])
        for t in every_y[1:]:
            pairs = [(device(0, 0, z, m), device(t, 0, z, m)) for z in range(planes) for m in range(lanes)]
            near2 = jnp.where(y == t, send(near2, pairs), near2)
        near12 = after(jnp.concatenate([halves[0], near2], axis=0), piece3)
        all12 = lane_gather(near12, [0], range(planes))
        (piece3,) = along_planes(piece3, [3])
        all12 = [near12] + [after(part, piece3) for part in all12[1:]]
        other12 = [core_send(part) for part in all12]
        *most3, last3 = plane_gather(piece3, [0])
        most3 = jnp.concatenate(most3, axis=0)
        other3 = core_send(most3)

        def whole_pieces(first):
            return [
                (mine, other, first * rows_here, rows_here, lane_places[d])
                for d, (mine, other) in enumerate(zip(all12, other12))
            ]

        (current,) = run(current, [(1, whole_pieces(0)), (2, whole_pieces(1))], [f32_rows])
        other_last3 = core_send(after(last3, current))
        pieces3 = [(most3, other3, i * cut, cut, place) for i, place in enumerate(tree_places[:-1])]
        pieces3.append((last3, other_last3, 0, cut, tree_places[-1]))
        (out,) = run(current, [(3, pieces3)], [(jnp.float32, 0, rows_here, True)])
        return out

    return on_device


def solution(mesh):
    placed = (P(AXES, None), P(AXES, None))
    on_device = make_on_device(mesh.shape["row"], mesh.shape["col"])
    return jax.shard_map(
        on_device, mesh=mesh, in_specs=placed, out_specs=P(AXES, None), check_vma=False
    )
```

```python
import functools

import jax
import jax.numpy as jnp
from jax import lax
from jax.experimental import pallas as pl
from jax.experimental.pallas import tpu as pltpu
from jax.sharding import PartitionSpec as P

NB = 2048
STEPS = 4
AXES = ("row", "col")
CORES = 2
TILE = 256
DEPTH = 512
KERNEL_VMEM = 40 * 1024 * 1024


def after(value, *others):
    return lax.optimization_barrier((value, *others))[0]


def step_kernel(terms, n_arrays, outs, where_am_i, active, *refs):
    current, panels = refs[:2]
    arrays = refs[2 : 2 + n_arrays]
    results = refs[2 + n_arrays : 2 + n_arrays + len(outs)]
    current_here, totals, panels_here, held, sems, piece_sems, current_sem, out_sems = refs[2 + n_arrays + len(outs) :]
    rows = current.shape[0]
    depth = min(DEPTH, NB)
    chunks = NB // depth
    here = where_am_i()

    def work():
        copies = []
        for t, (_, pieces) in enumerate(terms):
            for array, twin, first, size, place in pieces:
                start = pl.multiple_of(place(here) * size, size)

                def copy(source):
                    return pltpu.make_async_copy(
                        arrays[source].at[pl.ds(first, size), :],
                        held.at[t, pl.ds(start, size), :],
                        piece_sems.at[len(copies)],
                    )

                if twin is None:
                    copy(array).start()
                else:
                    pl.when(here.core == 0)(lambda: copy(array).start())
                    pl.when(here.core != 0)(lambda: copy(twin).start())
                copies.append(copy(array))

        def panel_copy(t, i):
            k = terms[t][0]
            return pltpu.make_async_copy(
                panels.at[:, pl.ds(k * NB + i * depth, depth)], panels_here.at[t, i], sems.at[t, i]
            )

        for t in range(len(terms)):
            for i in range(chunks):
                panel_copy(t, i).start()
        current_copy = pltpu.make_async_copy(current, current_here, current_sem)
        current_copy.start()
        for copy in copies:
            copy.wait()
        for t in range(len(terms)):
            for i in range(chunks):
                panel_copy(t, i).wait()
                part = jnp.dot(
                    panels_here[t, i], held[t, pl.ds(i * depth, depth), :], preferred_element_type=jnp.float32
                )
                totals[t] = part if i == 0 else totals[t] + part
        current_copy.wait()
        sent = []
        tile = min(TILE, rows)
        for i in range(rows // tile):
            at = pl.ds(i * tile, tile)
            value = current_here[at, :]
            for t, (k, _) in enumerate(terms):
                product = totals[t, at, :]
                value = jnp.where(here.block == k, product, value - product)
            for o, (dtype, first, size, far) in enumerate(outs):
                low, high = max(first, i * tile), min(first + size, (i + 1) * tile)
                if low < high:
                    part = value[low - i * tile : high - i * tile].astype(dtype)
                    if far:
                        current_here[at, :] = part
                        out = pltpu.make_async_copy(current_here.at[at, :], results[o].at[at, :], out_sems.at[i])
                        out.start()
                        sent.append(out)
                    else:
                        results[o][pl.ds(low - first, high - low), :] = part
        for out in sent:
            out.wait()

    if active is None:
        work()
    else:
        pl.when(active(here))(work)


def steps(current, factor_panels, terms, outs, where_am_i, active):
    rows, scenarios = current.shape
    arrays, plan = [], []

    def index(array):
        if array is None:
            return None
        for i, other in enumerate(arrays):
            if other is array:
                return i
        arrays.append(array)
        return len(arrays) - 1

    for k, pieces in terms:
        plan.append((k, tuple((index(a), index(b), first, size, place) for a, b, first, size, place in pieces)))
    n_terms = len(terms)
    depth = min(DEPTH, NB)
    n_pieces = sum(len(pieces) for _, pieces in terms)
    anywhere = pl.BlockSpec(memory_space=pl.ANY)
    return pl.pallas_call(
        functools.partial(step_kernel, tuple(plan), len(arrays), tuple(outs), where_am_i, active),
        in_specs=[anywhere] * (2 + len(arrays)),
        out_specs=[anywhere if out[3] else pl.BlockSpec(memory_space=pltpu.VMEM) for out in outs],
        out_shape=[jax.ShapeDtypeStruct((size, scenarios), dtype) for dtype, _, size, _ in outs],
        scratch_shapes=[
            pltpu.VMEM((rows, scenarios), jnp.float32),
            pltpu.VMEM((n_terms, rows, scenarios), jnp.float32),
            pltpu.VMEM((n_terms, NB // depth, rows, depth), jnp.bfloat16),
            pltpu.VMEM((n_terms, NB, scenarios), jnp.bfloat16),
            pltpu.SemaphoreType.DMA((n_terms, NB // depth)),
            pltpu.SemaphoreType.DMA((n_pieces,)),
            pltpu.SemaphoreType.DMA,
            pltpu.SemaphoreType.DMA((rows // min(TILE, rows),)),
        ],
        compiler_params=pltpu.CompilerParams(vmem_limit_bytes=KERNEL_VMEM),
        cost_estimate=pl.CostEstimate(
            flops=2 * rows * NB * scenarios * n_terms,
            bytes_accessed=8 * rows * scenarios,
            transcendentals=0,
        ),
    )(current, factor_panels, *arrays)


class Place:
    def __init__(self, n_col, lanes):
        row, col = lax.axis_index("row"), lax.axis_index("col")
        self.y, self.core = row // CORES, row % CORES
        self.plane, self.lane = col // lanes, col % lanes
        self.block = (row * n_col + col) // lanes


def make_on_device(n_row, n_col):
    def on_device(rhs_scen, factor_panels):
        rows_here = factor_panels.shape[0]
        lanes = NB // rows_here
        planes = n_col // lanes
        n_y = n_row // CORES
        members = lanes * n_y * CORES
        where_am_i = functools.partial(Place, n_col, lanes)
        here = where_am_i()
        y, core, plane = here.y, here.core, here.plane

        def device(y, core, plane, lane):
            return (y * CORES + core) * n_col + plane * lanes + lane

        def send(value, pairs):
            return lax.ppermute(value, AXES, pairs)

        def lane_gather(value, cores, zs, ys=range(n_y)):
            out = [value]
            for d in range(1, lanes):
                pairs = [
                    (device(t, c, z, (m + d) % lanes), device(t, c, z, m))
                    for t in ys for c in cores for z in zs for m in range(lanes)
                ]
                out.append(send(value, pairs))
            return out

        def y_gather(value, cores):
            out = [value]
            for d in range(1, n_y):
                pairs = [
                    (device((t + d) % n_y, c, z, m), device(t, c, z, m))
                    for t in range(n_y) for c in cores for z in range(planes) for m in range(lanes)
                ]
                out.append(send(value, pairs))
            return out

        def plane_gather(value, cores):
            first = lane_gather(value, cores, range(planes))
            far = y_gather(value, cores)[1:]
            return first + [part for got in far for part in lane_gather(got, cores, range(planes))]

        def ahead(own, k):
            return [
                send(own, [(device(0, 0, k, (m + d) % lanes), device(0, 0, k + 1, m)) for m in range(lanes)])
                for d in range(lanes)
            ]

        lane_places = [functools.partial(lambda d, at: (at.lane + d) % lanes, d) for d in range(lanes)]

        def scatter_y(cuts, sources):
            piece = cuts[0]
            for t in range(1, n_y):
                pairs = [(device(0, 0, k, m), device(t, 0, k, m)) for k in sources for m in range(lanes)]
                piece = jnp.where(y == t, send(cuts[t], pairs), piece)
            return piece

        def along_planes(piece, sources):
            got = []
            for d in range(1, planes):
                pairs = [
                    (device(t, 0, k, m), device(t, 0, (k + d) % planes, m))
                    for k in sources for t in range(n_y) for m in range(lanes)
                ]
                got.append(send(piece, pairs))
            out = []
            for k in sources:
                value = piece
                for d in range(1, planes):
                    value = jnp.where(plane == (k + d) % planes, got[d - 1], value)
                out.append(value)
            return out

        def core_send(value):
            return send(
                value,
                [
                    (device(t, 0, z, m), device(t, 1, z, m))
                    for t in range(n_y) for z in range(planes) for m in range(lanes)
                ],
            )

        tree_places = [
            functools.partial(lambda dy, dm, at: ((at.lane + dm) % lanes) * n_y + (at.y + dy) % n_y, dy, dm)
            for dy in range(n_y) for dm in range(lanes)
        ]

        extra = NB // members
        start_places = [
            functools.partial(
                lambda dc, dy, dm, at: ((at.y + dy) % n_y * CORES + (at.core + dc) % CORES) * lanes
                + (at.lane + dm) % lanes,
                dc, dy, dm,
            )
            for dc in range(CORES) for dy in range(n_y) for dm in range(lanes)
        ]
        first = rhs_scen[:, :NB].reshape(-1, n_row, 1, lanes, extra)
        first = jnp.broadcast_to(first, (first.shape[0], n_row, planes, lanes, extra))
        first = first.reshape(first.shape[0], n_row * n_col, extra)
        outgoing = jnp.concatenate(
            [rhs_scen.reshape(rhs_scen.shape[0], n_row * n_col, rows_here), first], axis=2
        )
        regrouped = lax.all_to_all(outgoing, AXES, split_axis=1, concat_axis=0, tiled=True)
        regrouped = regrouped.reshape(-1, rows_here + extra)
        current = jnp.transpose(regrouped[:, :rows_here]).astype(jnp.float32)
        piece = jnp.transpose(regrouped[:, rows_here:])
        both = range(CORES)
        whole = jnp.concatenate(plane_gather(piece, both), axis=0)
        other = send(
            whole,
            [
                (device(t, 1 - c, z, m), device(t, c, z, m))
                for t in range(n_y) for c in both for z in range(planes) for m in range(lanes)
            ],
        )
        per_core = members // CORES
        pieces = [
            (half, None, i * extra, extra, start_places[c * per_core + i])
            for c, half in enumerate([whole, other]) for i in range(per_core)
        ]

        def run(current, terms, outs, only=None):
            active = None if only is None else lambda at: at.block == only
            return steps(current, factor_panels, terms, outs, where_am_i, active)

        cut = rows_here // n_y
        f32_rows = (jnp.float32, 0, rows_here, False)
        own_rows = (jnp.bfloat16, 0, rows_here, False)
        own_cuts = [(jnp.bfloat16, t * cut, cut, False) for t in range(n_y)]

        def lane_pieces(parts):
            return [(part, None, 0, rows_here, lane_places[d]) for d, part in enumerate(parts)]

        current, own1 = run(current, [(0, pieces)], [f32_rows, own_rows])

        def to_plane(value, k, z):
            return send(value, [(device(0, 0, k, m), device(0, 0, z, m)) for m in range(lanes)])

        def to_y(value, t, zs):
            return send(value, [(device(0, 0, z, m), device(t, 0, z, m)) for z in zs for m in range(lanes)])

        hop1 = ahead(own1, 1)
        own1 = after(own1, hop1[0])
        got1 = {2: hop1[0], 3: to_plane(own1, 1, 3)}
        crossed = [
            send(own1, [(device(0, 0, 1, (m + d) % lanes), device(0, 0, 3, m)) for m in range(lanes)])
            for d in range(1, lanes)
        ]
        for z in range(planes):
            if z not in (1, 2, 3):
                got1[z] = to_plane(own1, 1, z)
        (own2,) = run(current, [(1, lane_pieces(hop1))], [own_rows], 2)
        hop2 = ahead(own2, 2)
        (chained,) = run(current, [(1, lane_pieces([got1[3], *crossed]))], [f32_rows], 3)
        cuts3 = list(run(chained, [(2, lane_pieces(hop2))], own_cuts, 3))

        near1 = own1
        for z, part in got1.items():
            near1 = jnp.where(plane == z, part, near1)
        near1 = after(near1, chained)
        for t in range(1, n_y):
            near1 = jnp.where(y == t, to_y(near1, t, range(planes)), near1)
        own2 = after(own2, chained)
        cuts2 = [own2[t * cut : (t + 1) * cut] for t in range(n_y)]
        cuts2 = cuts2[:1] + [to_y(cuts2[t], t, [2]) for t in range(1, n_y)]

        cuts3 = cuts3[:1] + [to_y(cuts3[t], t, [3]) for t in range(1, n_y)]
        piece = jnp.where(plane == 2, cuts2[0], cuts3[0])
        for t in range(1, n_y):
            piece = jnp.where(y == t, jnp.where(plane == 2, cuts2[t], cuts3[t]), piece)
        near1 = after(near1, piece)
        all1 = lane_gather(near1, [0], range(planes))
        piece = jnp.concatenate(along_planes(piece, [2, 3]), axis=0)
        other1 = [core_send(part) for part in all1]
        pieces1 = [
            (mine, other, 0, rows_here, lane_places[d]) for d, (mine, other) in enumerate(zip(all1, other1))
        ]
        (current,) = run(current, [(1, pieces1)], [f32_rows])
        near = lane_gather(piece, [0], range(planes))
        far = [after(got, current) for got in y_gather(piece, [0])[1:]]
        most = jnp.concatenate(near + far, axis=0)
        last = [part for got in far for part in lane_gather(got, [0], range(planes))[1:]]
        other_most = core_send(most)
        last = last[0] if len(last) == 1 else jnp.concatenate(last, axis=0)
        other_last = core_send(last)
        places_most = tree_places[:lanes] + tree_places[lanes::lanes]
        places_last = [p for i, p in enumerate(tree_places) if i >= lanes and i % lanes]

        def tree_pieces(first):
            return [
                (mine, other, i * 2 * cut + first, cut, place)
                for mine, other, places in ((most, other_most, places_most), (last, other_last, places_last))
                for i, place in enumerate(places)
            ]

        (out,) = run(
            current, [(2, tree_pieces(0)), (3, tree_pieces(cut))], [(jnp.float32, 0, rows_here, True)]
        )
        return out

    return on_device


def solution(mesh):
    placed = (P(AXES, None), P(AXES, None))
    on_device = make_on_device(mesh.shape["row"], mesh.shape["col"])
    return jax.shard_map(
        on_device, mesh=mesh, in_specs=placed, out_specs=P(AXES, None), check_vma=False
    )
```

```python
import functools

import jax
import jax.numpy as jnp
from jax import lax
from jax.experimental import pallas as pl
from jax.experimental.pallas import tpu as pltpu
from jax.sharding import PartitionSpec as P

NB = 2048
STEPS = 4
AXES = ("row", "col")
CORES = 2
DEPTH = 512
KERNEL_VMEM = 40 * 1024 * 1024


def after(value, *others):
    return lax.optimization_barrier((value, *others))[0]


class Place:
    def __init__(self, n_col, lanes):
        row, col = lax.axis_index("row"), lax.axis_index("col")
        self.y, self.core = row // CORES, row % CORES
        self.plane, self.lane = col // lanes, col % lanes
        self.block = (row * n_col + col) // lanes


def step_kernel(terms, handed, n_arrays, outs, where_am_i, only, *refs):
    current, panels = refs[:2]
    arrays = refs[2 : 2 + n_arrays]
    results = refs[2 + n_arrays : 2 + n_arrays + len(outs)]
    current_here, panels_here, held, sems, piece_sems, current_sem, out_sem = refs[2 + n_arrays + len(outs) :]
    rows = current.shape[0]
    depth = min(DEPTH, NB)
    chunks = NB // depth
    here = where_am_i()

    def work():
        copies = []
        for t, (_, pieces) in enumerate(terms):
            for array, first, size, place in pieces:
                start = pl.multiple_of(place(here) * size, size)
                copy = pltpu.make_async_copy(
                    arrays[array].at[pl.ds(first, size), :],
                    held.at[t, pl.ds(start, size), :],
                    piece_sems.at[len(copies)],
                )
                copy.start()
                copies.append(copy)

        def panel_copy(t, i):
            k = terms[t][0]
            return pltpu.make_async_copy(
                panels.at[:, pl.ds(k * NB + i * depth, depth)], panels_here.at[t, i], sems.at[t, i]
            )

        for t in range(len(terms)):
            for i in range(chunks):
                panel_copy(t, i).start()
        current_copy = pltpu.make_async_copy(current, current_here, current_sem)
        current_copy.start()
        for copy in copies:
            copy.wait()
        current_copy.wait()
        for t, (k, _) in enumerate(terms):
            own = here.block == k
            for i in range(chunks):
                panel_copy(t, i).wait()
                part = jnp.dot(
                    panels_here[t, i], held[t, pl.ds(i * depth, depth), :], preferred_element_type=jnp.float32
                )
                now = current_here[...]
                current_here[...] = jnp.where(own, part if i == 0 else now + part, now - part)
        sent = []
        for o, (dtype, first, size, far) in enumerate(outs):
            if far:
                sent.append(pltpu.make_async_copy(current_here.at[pl.ds(first, size), :], results[o], out_sem))
                sent[-1].start()
            else:
                results[o][...] = current_here[pl.ds(first, size), :].astype(dtype)
        for out in sent:
            out.wait()

    if only is None:
        work()
    else:
        pl.when(here.block == only)(work)
    for block, array in handed:

        def hand(array=array):
            copies = [
                pltpu.make_async_copy(arrays[array].at[pl.ds(first, size), :], results[o], piece_sems.at[o])
                for o, (_, first, size, _) in enumerate(outs)
            ]
            for copy in copies:
                copy.start()
            for copy in copies:
                copy.wait()

        pl.when(here.block == block)(hand)


def steps(current, factor_panels, terms, outs, where_am_i, only=None, handed=()):
    rows, scenarios = current.shape
    arrays = []

    def index(array):
        for i, other in enumerate(arrays):
            if other is array:
                return i
        arrays.append(array)
        return len(arrays) - 1

    plan = tuple(
        (k, tuple((index(array), first, size, place) for array, first, size, place in pieces)) for k, pieces in terms
    )
    handed = tuple((block, index(array)) for block, array in handed)
    n_terms = len(terms)
    depth = min(DEPTH, NB)
    n_pieces = max(sum(len(pieces) for _, pieces in terms), len(outs))
    anywhere = pl.BlockSpec(memory_space=pl.ANY)
    return pl.pallas_call(
        functools.partial(step_kernel, plan, handed, len(arrays), tuple(outs), where_am_i, only),
        in_specs=[anywhere] * (2 + len(arrays)),
        out_specs=[anywhere if out[3] else pl.BlockSpec(memory_space=pltpu.VMEM) for out in outs],
        out_shape=[jax.ShapeDtypeStruct((size, scenarios), dtype) for dtype, _, size, _ in outs],
        scratch_shapes=[
            pltpu.VMEM((rows, scenarios), jnp.float32),
            pltpu.VMEM((n_terms, NB // depth, rows, depth), jnp.bfloat16),
            pltpu.VMEM((n_terms, NB, scenarios), jnp.bfloat16),
            pltpu.SemaphoreType.DMA((n_terms, NB // depth)),
            pltpu.SemaphoreType.DMA((n_pieces,)),
            pltpu.SemaphoreType.DMA,
            pltpu.SemaphoreType.DMA,
        ],
        compiler_params=pltpu.CompilerParams(vmem_limit_bytes=KERNEL_VMEM),
        cost_estimate=pl.CostEstimate(
            flops=2 * rows * NB * scenarios * n_terms,
            bytes_accessed=8 * rows * scenarios,
            transcendentals=0,
        ),
    )(current, factor_panels, *arrays)


def make_on_device(n_row, n_col):
    def on_device(rhs_scen, factor_panels):
        rows_here = factor_panels.shape[0]
        lanes = NB // rows_here
        planes = n_col // lanes
        n_y = n_row // CORES
        members = n_row * lanes
        where_am_i = functools.partial(Place, n_col, lanes)
        here = where_am_i()
        core, plane = here.core, here.plane

        def device(y, core, plane, lane):
            return (y * CORES + core) * n_col + plane * lanes + lane

        def send(value, pairs):
            return lax.ppermute(value, AXES, pairs)

        def run(current, terms, outs, only=None, handed=()):
            return steps(current, factor_panels, terms, outs, where_am_i, only, handed)

        def ahead(own, k):
            return [
                send(own, [(device(0, 0, k, (m + d) % lanes), device(0, 0, k + 1, m)) for m in range(lanes)])
                for d in range(lanes)
            ]

        along_x = [(0, d) for d in range(1, lanes)]
        along_y = [(d, 0) for d in range(1, n_y)]
        first_0, first_1 = along_x + along_y, along_y + along_x
        across = [(dy, dm) for dy, _ in along_y for _, dm in along_x]
        offsets = [((0, 0), (0, 0)), *zip(first_0, first_1), *zip(across, across)]

        def plane_gather(value):
            def pairs(c, step):
                return [
                    (device((t + step[0]) % n_y, c, z, (m + step[1]) % lanes), device(t, c, z, m))
                    for t in range(n_y) for z in range(planes) for m in range(lanes)
                ]

            got = [send(value, pairs(0, a) + pairs(1, b)) for a, b in zip(first_0, first_1)]
            last = []
            for dy, dm in across:
                a, b = first_0.index((dy, 0)), first_1.index((0, dm))
                payload = got[a] if a == b else jnp.where(core == 0, got[a], got[b])
                last.append(send(payload, pairs(0, (0, dm)) + pairs(1, (dy, 0))))
            return jnp.concatenate([value, *got, *last], axis=0)

        def core_exchange(value):
            pairs = [
                (device(t, 1 - c, z, m), device(t, c, z, m))
                for t in range(n_y) for c in range(CORES) for z in range(planes) for m in range(lanes)
            ]
            return send(value, pairs)

        def gathered_pieces(mine, other, first, size, stride, number):
            def place(offset, own, at):
                c = at.core if own else 1 - at.core
                a, b = (number((at.y + dy) % n_y, c, (at.lane + dm) % lanes) for dy, dm in offset)
                return a if offset[0] == offset[1] else jnp.where(c == 0, a, b)

            return [
                (array, i * stride + first, size, functools.partial(place, offset, array is mine))
                for array in (mine, other) for i, offset in enumerate(offsets)
            ]

        def lane_pieces(parts):
            return [
                (part, 0, rows_here, functools.partial(lambda d, at: (at.lane + d) % lanes, d))
                for d, part in enumerate(parts)
            ]

        f32_rows = (jnp.float32, 0, rows_here, False)
        own_rows = (jnp.bfloat16, 0, rows_here, False)
        cut = rows_here // n_row
        own_cuts = [(jnp.bfloat16, t * cut, cut, False) for t in range(n_row)]

        extra = NB // members
        first = rhs_scen[:, :NB].reshape(-1, n_row, 1, lanes, extra)
        first = jnp.broadcast_to(first, (first.shape[0], n_row, planes, lanes, extra))
        first = first.reshape(first.shape[0], n_row * n_col, extra)
        outgoing = jnp.concatenate(
            [rhs_scen.reshape(rhs_scen.shape[0], n_row * n_col, rows_here), first], axis=2
        )
        regrouped = lax.all_to_all(outgoing, AXES, split_axis=1, concat_axis=0, tiled=True)
        regrouped = regrouped.reshape(-1, rows_here + extra)
        current = jnp.transpose(regrouped[:, :rows_here]).astype(jnp.float32)
        whole = plane_gather(jnp.transpose(regrouped[:, rows_here:]))
        pieces = gathered_pieces(
            whole, core_exchange(whole), 0, extra, extra, lambda y, c, m: (y * CORES + c) * lanes + m
        )
        current, own1 = run(current, [(0, pieces)], [f32_rows, own_rows])

        hop1 = ahead(own1, 1)
        start1 = after(own1, hop1[0])
        at_3 = [
            send(start1, [(device(0, 0, 1, (m + d) % lanes), device(0, 0, 3, m)) for m in range(lanes)])
            for d in range(lanes)
        ]
        (own2,) = run(current, [(1, lane_pieces(hop1))], [own_rows], 2)
        hop2 = ahead(own2, 2)
        (chained,) = run(current, [(1, lane_pieces(at_3))], [f32_rows], 3)
        cuts = run(chained, [(2, lane_pieces(hop2))], own_cuts, 3, [(1, own1), (2, own2)])

        piece = cuts[0]
        for t in range(1, n_row):
            pairs = [
                (device(0, 0, k, m), device(t // CORES, t % CORES, k, m)) for k in range(1, STEPS) for m in range(lanes)
            ]
            piece = jnp.where(here.y * CORES + core == t, send(cuts[t], pairs), piece)
        got = [
            send(
                piece,
                [
                    (device(t, c, k, m), device(t, c, (k + d) % planes, m))
                    for k in range(1, STEPS) for t in range(n_y) for c in range(CORES) for m in range(lanes)
                ],
            )
            for d in range(1, planes)
        ]
        three = []
        for k in range(1, STEPS):
            value = piece
            for d in range(1, planes):
                value = jnp.where(plane == (k + d) % planes, got[d - 1], value)
            three.append(value)
        whole = plane_gather(jnp.concatenate(three, axis=0))
        other = core_exchange(whole)
        terms = [
            (
                k,
                gathered_pieces(
                    whole, other, (k - 1) * cut, cut, (STEPS - 1) * cut, lambda y, c, m: m * n_row + y * CORES + c
                ),
            )
            for k in range(1, STEPS)
        ]
        (out,) = run(current, terms, [(jnp.float32, 0, rows_here, True)])
        return out

    return on_device


def solution(mesh):
    placed = (P(AXES, None), P(AXES, None))
    on_device = make_on_device(mesh.shape["row"], mesh.shape["col"])
    return jax.shard_map(
        on_device, mesh=mesh, in_specs=placed, out_specs=P(AXES, None), check_vma=False
    )
```

```python
import functools

import jax
import jax.numpy as jnp
from jax import lax
from jax.experimental import pallas as pl
from jax.experimental.pallas import tpu as pltpu
from jax.sharding import PartitionSpec as P

NB = 2048
STEPS = 4
AXES = ("row", "col")
CORES = 2
DEPTH = 512
IN_FLIGHT = 3
KERNEL_VMEM = 40 * 1024 * 1024


def after(value, *others):
    return lax.optimization_barrier((value, *others))[0]


class Place:
    def __init__(self, n_col, lanes):
        row, col = lax.axis_index("row"), lax.axis_index("col")
        self.y, self.core = row // CORES, row % CORES
        self.plane, self.lane = col // lanes, col % lanes
        self.block = (row * n_col + col) // lanes


def step_kernel(terms, handed, n_arrays, outs, where_am_i, only, *refs):
    current, panels = refs[:2]
    arrays = refs[2 : 2 + n_arrays]
    results = refs[2 + n_arrays : 2 + n_arrays + len(outs)]
    current_here, panels_here, held, sems, piece_sems, current_sem, out_sem = refs[2 + n_arrays + len(outs) :]
    rows = current.shape[0]
    depth = min(DEPTH, NB)
    chunks = NB // depth
    here = where_am_i()

    def work():
        copies = [[] for _ in terms]
        for t, (_, pieces) in enumerate(terms):
            for array, first, size, place in pieces:
                start = pl.multiple_of(place(here) * size, size)
                copies[t].append(
                    pltpu.make_async_copy(
                        arrays[array].at[pl.ds(first, size), :],
                        held.at[t, pl.ds(start, size), :],
                        piece_sems.at[sum(len(c) for c in copies)],
                    )
                )

        def panel_copy(t, i):
            k = terms[t][0]
            return pltpu.make_async_copy(
                panels.at[:, pl.ds(k * NB + i * depth, depth)], panels_here.at[t, i], sems.at[t, i]
            )

        def load(t, i):
            if i == 0:
                for copy in copies[t]:
                    copy.start()
            panel_copy(t, i).start()

        order = [(t, i) for t in range(len(terms)) for i in range(chunks)]
        current_copy = pltpu.make_async_copy(current, current_here, current_sem)
        current_copy.start()
        for t, i in order[:IN_FLIGHT]:
            load(t, i)
        current_copy.wait()
        for n, (t, i) in enumerate(order):
            if i == 0:
                for copy in copies[t]:
                    copy.wait()
            panel_copy(t, i).wait()
            if n + IN_FLIGHT < len(order):
                load(*order[n + IN_FLIGHT])
            part = jnp.dot(
                panels_here[t, i], held[t, pl.ds(i * depth, depth), :], preferred_element_type=jnp.float32
            )
            own = here.block == terms[t][0]
            now = current_here[...]
            current_here[...] = jnp.where(own, part if i == 0 else now + part, now - part)
        sent = []
        for o, (dtype, first, size, far) in enumerate(outs):
            if far:
                sent.append(pltpu.make_async_copy(current_here.at[pl.ds(first, size), :], results[o], out_sem))
                sent[-1].start()
            else:
                results[o][...] = current_here[pl.ds(first, size), :].astype(dtype)
        for out in sent:
            out.wait()

    if only is None:
        work()
    else:
        pl.when(here.block == only)(work)
    for block, array in handed:

        def hand(array=array):
            copies = [
                pltpu.make_async_copy(arrays[array].at[pl.ds(first, size), :], results[o], piece_sems.at[o])
                for o, (_, first, size, _) in enumerate(outs)
            ]
            for copy in copies:
                copy.start()
            for copy in copies:
                copy.wait()

        pl.when(here.block == block)(hand)


def steps(current, factor_panels, terms, outs, where_am_i, only=None, handed=()):
    rows, scenarios = current.shape
    arrays = []

    def index(array):
        for i, other in enumerate(arrays):
            if other is array:
                return i
        arrays.append(array)
        return len(arrays) - 1

    plan = tuple(
        (k, tuple((index(array), first, size, place) for array, first, size, place in pieces)) for k, pieces in terms
    )
    handed = tuple((block, index(array)) for block, array in handed)
    n_terms = len(terms)
    depth = min(DEPTH, NB)
    n_pieces = max(sum(len(pieces) for _, pieces in terms), len(outs))
    anywhere = pl.BlockSpec(memory_space=pl.ANY)
    return pl.pallas_call(
        functools.partial(step_kernel, plan, handed, len(arrays), tuple(outs), where_am_i, only),
        in_specs=[anywhere] * (2 + len(arrays)),
        out_specs=[anywhere if out[3] else pl.BlockSpec(memory_space=pltpu.VMEM) for out in outs],
        out_shape=[jax.ShapeDtypeStruct((size, scenarios), dtype) for dtype, _, size, _ in outs],
        scratch_shapes=[
            pltpu.VMEM((rows, scenarios), jnp.float32),
            pltpu.VMEM((n_terms, NB // depth, rows, depth), jnp.bfloat16),
            pltpu.VMEM((n_terms, NB, scenarios), jnp.bfloat16),
            pltpu.SemaphoreType.DMA((n_terms, NB // depth)),
            pltpu.SemaphoreType.DMA((n_pieces,)),
            pltpu.SemaphoreType.DMA,
            pltpu.SemaphoreType.DMA,
        ],
        compiler_params=pltpu.CompilerParams(vmem_limit_bytes=KERNEL_VMEM),
        cost_estimate=pl.CostEstimate(
            flops=2 * rows * NB * scenarios * n_terms,
            bytes_accessed=8 * rows * scenarios,
            transcendentals=0,
        ),
    )(current, factor_panels, *arrays)


def make_on_device(n_row, n_col):
    def on_device(rhs_scen, factor_panels):
        rows_here = factor_panels.shape[0]
        lanes = NB // rows_here
        planes = n_col // lanes
        n_y = n_row // CORES
        members = n_row * lanes
        where_am_i = functools.partial(Place, n_col, lanes)
        here = where_am_i()
        core, plane = here.core, here.plane

        def device(y, core, plane, lane):
            return (y * CORES + core) * n_col + plane * lanes + lane

        def send(value, pairs):
            return lax.ppermute(value, AXES, pairs)

        def run(current, terms, outs, only=None, handed=()):
            return steps(current, factor_panels, terms, outs, where_am_i, only, handed)

        def ahead(own, k):
            return [
                send(own, [(device(0, 0, k, (m + d) % lanes), device(0, 0, k + 1, m)) for m in range(lanes)])
                for d in range(lanes)
            ]

        along_x = [(0, d) for d in range(1, lanes)]
        along_y = [(d, 0) for d in range(1, n_y)]
        first_0, first_1 = along_x + along_y, along_y + along_x
        across = [(dy, dm) for dy, _ in along_y for _, dm in along_x]
        offsets = [((0, 0), (0, 0)), *zip(first_0, first_1), *zip(across, across)]

        def plane_gather(value):
            def pairs(c, step):
                return [
                    (device((t + step[0]) % n_y, c, z, (m + step[1]) % lanes), device(t, c, z, m))
                    for t in range(n_y) for z in range(planes) for m in range(lanes)
                ]

            got = [send(value, pairs(0, a) + pairs(1, b)) for a, b in zip(first_0, first_1)]
            last = []
            for dy, dm in across:
                a, b = first_0.index((dy, 0)), first_1.index((0, dm))
                payload = got[a] if a == b else jnp.where(core == 0, got[a], got[b])
                last.append(send(payload, pairs(0, (0, dm)) + pairs(1, (dy, 0))))
            return jnp.concatenate([value, *got, *last], axis=0)

        def core_exchange(value):
            pairs = [
                (device(t, 1 - c, z, m), device(t, c, z, m))
                for t in range(n_y) for c in range(CORES) for z in range(planes) for m in range(lanes)
            ]
            return send(value, pairs)

        def gathered_pieces(mine, other, first, size, stride, number):
            def place(offset, own, at):
                c = at.core if own else 1 - at.core
                a, b = (number((at.y + dy) % n_y, c, (at.lane + dm) % lanes) for dy, dm in offset)
                return a if offset[0] == offset[1] else jnp.where(c == 0, a, b)

            return [
                (array, i * stride + first, size, functools.partial(place, offset, array is mine))
                for array in (mine, other) for i, offset in enumerate(offsets)
            ]

        def lane_pieces(parts):
            return [
                (part, 0, rows_here, functools.partial(lambda d, at: (at.lane + d) % lanes, d))
                for d, part in enumerate(parts)
            ]

        f32_rows = (jnp.float32, 0, rows_here, False)
        own_rows = (jnp.bfloat16, 0, rows_here, False)
        cut = rows_here // n_row
        own_cuts = [(jnp.bfloat16, t * cut, cut, False) for t in range(n_row)]

        extra = NB // members
        first = rhs_scen[:, :NB].reshape(-1, n_row, 1, lanes, extra)
        first = jnp.broadcast_to(first, (first.shape[0], n_row, planes, lanes, extra))
        first = first.reshape(first.shape[0], n_row * n_col, extra)
        outgoing = jnp.concatenate(
            [rhs_scen.reshape(rhs_scen.shape[0], n_row * n_col, rows_here), first], axis=2
        )
        regrouped = lax.all_to_all(outgoing, AXES, split_axis=1, concat_axis=0, tiled=True)
        regrouped = regrouped.reshape(-1, rows_here + extra)
        current = jnp.transpose(regrouped[:, :rows_here]).astype(jnp.float32)
        whole = plane_gather(jnp.transpose(regrouped[:, rows_here:]))
        pieces = gathered_pieces(
            whole, core_exchange(whole), 0, extra, extra, lambda y, c, m: (y * CORES + c) * lanes + m
        )
        current, own1 = run(current, [(0, pieces)], [f32_rows, own_rows])

        hop1 = ahead(own1, 1)
        start1 = after(own1, hop1[0])
        at_3 = [
            send(start1, [(device(0, 0, 1, (m + d) % lanes), device(0, 0, 3, m)) for m in range(lanes)])
            for d in range(lanes)
        ]
        (own2,) = run(current, [(1, lane_pieces(hop1))], [own_rows], 2)
        hop2 = ahead(own2, 2)
        (chained,) = run(current, [(1, lane_pieces(at_3))], [f32_rows], 3)
        cuts = run(chained, [(2, lane_pieces(hop2))], own_cuts, 3, [(1, own1), (2, own2)])

        piece = cuts[0]
        for t in range(1, n_row):
            pairs = [
                (device(0, 0, k, m), device(t // CORES, t % CORES, k, m)) for k in range(1, STEPS) for m in range(lanes)
            ]
            piece = jnp.where(here.y * CORES + core == t, send(cuts[t], pairs), piece)
        got = [
            send(
                piece,
                [
                    (device(t, c, k, m), device(t, c, (k + d) % planes, m))
                    for k in range(1, STEPS) for t in range(n_y) for c in range(CORES) for m in range(lanes)
                ],
            )
            for d in range(1, planes)
        ]
        three = []
        for k in range(1, STEPS):
            value = piece
            for d in range(1, planes):
                value = jnp.where(plane == (k + d) % planes, got[d - 1], value)
            three.append(value)
        whole = plane_gather(jnp.concatenate(three, axis=0))
        other = core_exchange(whole)
        terms = [
            (
                k,
                gathered_pieces(
                    whole, other, (k - 1) * cut, cut, (STEPS - 1) * cut, lambda y, c, m: m * n_row + y * CORES + c
                ),
            )
            for k in range(1, STEPS)
        ]
        (out,) = run(current, terms, [(jnp.float32, 0, rows_here, True)])
        return out

    return on_device


def solution(mesh):
    placed = (P(AXES, None), P(AXES, None))
    on_device = make_on_device(mesh.shape["row"], mesh.shape["col"])
    return jax.shard_map(
        on_device, mesh=mesh, in_specs=placed, out_specs=P(AXES, None), check_vma=False
    )
```

```python
import functools

import jax
import jax.numpy as jnp
from jax import lax
from jax.experimental import pallas as pl
from jax.experimental.pallas import tpu as pltpu
from jax.sharding import PartitionSpec as P

NB = 2048
STEPS = 4
AXES = ("row", "col")
CORES = 2
TILE = 256
IN_FLIGHT = 3
KERNEL_VMEM = 40 * 1024 * 1024


def after(value, *others):
    return lax.optimization_barrier((value, *others))[0]


class Place:
    def __init__(self, n_col, lanes):
        row, col = lax.axis_index("row"), lax.axis_index("col")
        self.y, self.core = row // CORES, row % CORES
        self.plane, self.lane = col // lanes, col % lanes
        self.block = (row * n_col + col) // lanes


def step_kernel(terms, handed, n_arrays, outs, where_am_i, only, *refs):
    current, panels = refs[:2]
    arrays = refs[2 : 2 + n_arrays]
    results = refs[2 + n_arrays : 2 + n_arrays + len(outs)]
    current_here, panels_here, held, sems, piece_sems, out_sems = refs[2 + n_arrays + len(outs) :]
    rows = current.shape[0]
    tile = min(TILE, rows)
    here = where_am_i()

    def work():
        copies = [[] for _ in terms]
        for t, (_, pieces) in enumerate(terms):
            for array, first, size, place in pieces:
                start = pl.multiple_of(place(here) * size, size)
                copies[t].append(
                    pltpu.make_async_copy(
                        arrays[array].at[pl.ds(first, size), :],
                        held.at[t, pl.ds(start, size), :],
                        piece_sems.at[sum(len(c) for c in copies)],
                    )
                )

        def panel_copy(t, i):
            k = terms[t][0]
            return pltpu.make_async_copy(
                panels.at[pl.ds(i * tile, tile), pl.ds(k * NB, NB)], panels_here.at[t, i], sems.at[t, i]
            )

        def current_copy(i):
            at = pl.ds(i * tile, tile)
            return pltpu.make_async_copy(current.at[at, :], current_here.at[at, :], sems.at[len(terms), i])

        def load(t, i):
            if i == 0:
                for copy in copies[t]:
                    copy.start()
            panel_copy(t, i).start()
            if t == 0:
                current_copy(i).start()

        order = [(t, i) for i in range(rows // tile) for t in range(len(terms))]
        in_flight = max(IN_FLIGHT, len(terms))
        for t, i in order[:in_flight]:
            load(t, i)
        sent = []
        for n, (t, i) in enumerate(order):
            at = pl.ds(i * tile, tile)
            if i == 0:
                for copy in copies[t]:
                    copy.wait()
            if t == 0:
                current_copy(i).wait()
                value = current_here[at, :]
            panel_copy(t, i).wait()
            if n + in_flight < len(order):
                load(*order[n + in_flight])
            product = jnp.dot(panels_here[t, i], held[t], preferred_element_type=jnp.float32)
            value = jnp.where(here.block == terms[t][0], product, value - product)
            if t < len(terms) - 1:
                continue
            for o, (dtype, first, size, far) in enumerate(outs):
                low, high = max(first, i * tile), min(first + size, (i + 1) * tile)
                if low < high:
                    part = value[low - i * tile : high - i * tile].astype(dtype)
                    if far:
                        current_here[at, :] = part
                        sent.append(pltpu.make_async_copy(current_here.at[at, :], results[o].at[at, :], out_sems.at[i]))
                        sent[-1].start()
                    else:
                        results[o][pl.ds(low - first, high - low), :] = part
        for out in sent:
            out.wait()

    if only is None:
        work()
    else:
        pl.when(here.block == only)(work)
    for block, array in handed:

        def hand(array=array):
            copies = [
                pltpu.make_async_copy(arrays[array].at[pl.ds(first, size), :], results[o], piece_sems.at[o])
                for o, (_, first, size, _) in enumerate(outs)
            ]
            for copy in copies:
                copy.start()
            for copy in copies:
                copy.wait()

        pl.when(here.block == block)(hand)


def steps(current, factor_panels, terms, outs, where_am_i, only=None, handed=()):
    rows, scenarios = current.shape
    arrays = []

    def index(array):
        for i, other in enumerate(arrays):
            if other is array:
                return i
        arrays.append(array)
        return len(arrays) - 1

    plan = tuple(
        (k, tuple((index(array), first, size, place) for array, first, size, place in pieces)) for k, pieces in terms
    )
    handed = tuple((block, index(array)) for block, array in handed)
    n_terms = len(terms)
    tile = min(TILE, rows)
    n_pieces = max(sum(len(pieces) for _, pieces in terms), len(outs))
    anywhere = pl.BlockSpec(memory_space=pl.ANY)
    return pl.pallas_call(
        functools.partial(step_kernel, plan, handed, len(arrays), tuple(outs), where_am_i, only),
        in_specs=[anywhere] * (2 + len(arrays)),
        out_specs=[anywhere if out[3] else pl.BlockSpec(memory_space=pltpu.VMEM) for out in outs],
        out_shape=[jax.ShapeDtypeStruct((size, scenarios), dtype) for dtype, _, size, _ in outs],
        scratch_shapes=[
            pltpu.VMEM((rows, scenarios), jnp.float32),
            pltpu.VMEM((n_terms, rows // tile, tile, NB), jnp.bfloat16),
            pltpu.VMEM((n_terms, NB, scenarios), jnp.bfloat16),
            pltpu.SemaphoreType.DMA((n_terms + 1, rows // tile)),
            pltpu.SemaphoreType.DMA((n_pieces,)),
            pltpu.SemaphoreType.DMA((rows // tile,)),
        ],
        compiler_params=pltpu.CompilerParams(vmem_limit_bytes=KERNEL_VMEM),
        cost_estimate=pl.CostEstimate(
            flops=2 * rows * NB * scenarios * n_terms,
            bytes_accessed=8 * rows * scenarios,
            transcendentals=0,
        ),
    )(current, factor_panels, *arrays)


def make_on_device(n_row, n_col):
    def on_device(rhs_scen, factor_panels):
        rows_here = factor_panels.shape[0]
        lanes = NB // rows_here
        planes = n_col // lanes
        n_y = n_row // CORES
        members = n_row * lanes
        where_am_i = functools.partial(Place, n_col, lanes)
        here = where_am_i()
        core, plane = here.core, here.plane

        def device(y, core, plane, lane):
            return (y * CORES + core) * n_col + plane * lanes + lane

        def send(value, pairs):
            return lax.ppermute(value, AXES, pairs)

        def run(current, terms, outs, only=None, handed=()):
            return steps(current, factor_panels, terms, outs, where_am_i, only, handed)

        def ahead(own, k):
            return [
                send(own, [(device(0, 0, k, (m + d) % lanes), device(0, 0, k + 1, m)) for m in range(lanes)])
                for d in range(lanes)
            ]

        along_x = [(0, d) for d in range(1, lanes)]
        along_y = [(d, 0) for d in range(1, n_y)]
        first_0, first_1 = along_x + along_y, along_y + along_x
        across = [(dy, dm) for dy, _ in along_y for _, dm in along_x]
        offsets = [((0, 0), (0, 0)), *zip(first_0, first_1), *zip(across, across)]

        def plane_gather(value):
            def pairs(c, step):
                return [
                    (device((t + step[0]) % n_y, c, z, (m + step[1]) % lanes), device(t, c, z, m))
                    for t in range(n_y) for z in range(planes) for m in range(lanes)
                ]

            got = [send(value, pairs(0, a) + pairs(1, b)) for a, b in zip(first_0, first_1)]
            last = []
            for dy, dm in across:
                a, b = first_0.index((dy, 0)), first_1.index((0, dm))
                payload = got[a] if a == b else jnp.where(core == 0, got[a], got[b])
                last.append(send(payload, pairs(0, (0, dm)) + pairs(1, (dy, 0))))
            return jnp.concatenate([value, *got, *last], axis=0)

        def core_exchange(value):
            pairs = [
                (device(t, 1 - c, z, m), device(t, c, z, m))
                for t in range(n_y) for c in range(CORES) for z in range(planes) for m in range(lanes)
            ]
            return send(value, pairs)

        def gathered_pieces(mine, other, first, size, stride, number):
            def place(offset, own, at):
                c = at.core if own else 1 - at.core
                a, b = (number((at.y + dy) % n_y, c, (at.lane + dm) % lanes) for dy, dm in offset)
                return a if offset[0] == offset[1] else jnp.where(c == 0, a, b)

            return [
                (array, i * stride + first, size, functools.partial(place, offset, array is mine))
                for array in (mine, other) for i, offset in enumerate(offsets)
            ]

        def lane_pieces(parts):
            return [
                (part, 0, rows_here, functools.partial(lambda d, at: (at.lane + d) % lanes, d))
                for d, part in enumerate(parts)
            ]

        f32_rows = (jnp.float32, 0, rows_here, False)
        own_rows = (jnp.bfloat16, 0, rows_here, False)
        cut = rows_here // n_row
        own_cuts = [(jnp.bfloat16, t * cut, cut, False) for t in range(n_row)]

        extra = NB // members
        first = rhs_scen[:, :NB].reshape(-1, n_row, 1, lanes, extra)
        first = jnp.broadcast_to(first, (first.shape[0], n_row, planes, lanes, extra))
        first = first.reshape(first.shape[0], n_row * n_col, extra)
        outgoing = jnp.concatenate(
            [rhs_scen.reshape(rhs_scen.shape[0], n_row * n_col, rows_here), first], axis=2
        )
        regrouped = lax.all_to_all(outgoing, AXES, split_axis=1, concat_axis=0, tiled=True)
        regrouped = regrouped.reshape(-1, rows_here + extra)
        current = jnp.transpose(regrouped[:, :rows_here]).astype(jnp.float32)
        whole = plane_gather(jnp.transpose(regrouped[:, rows_here:]))
        pieces = gathered_pieces(
            whole, core_exchange(whole), 0, extra, extra, lambda y, c, m: (y * CORES + c) * lanes + m
        )
        current, own1 = run(current, [(0, pieces)], [f32_rows, own_rows])

        hop1 = ahead(own1, 1)
        start1 = after(own1, hop1[0])
        at_3 = [
            send(start1, [(device(0, 0, 1, (m + d) % lanes), device(0, 0, 3, m)) for m in range(lanes)])
            for d in range(lanes)
        ]
        (own2,) = run(current, [(1, lane_pieces(hop1))], [own_rows], 2)
        hop2 = ahead(own2, 2)
        (chained,) = run(current, [(1, lane_pieces(at_3))], [f32_rows], 3)
        cuts = run(chained, [(2, lane_pieces(hop2))], own_cuts, 3, [(1, own1), (2, own2)])

        piece = cuts[0]
        for t in range(1, n_row):
            pairs = [
                (device(0, 0, k, m), device(t // CORES, t % CORES, k, m)) for k in range(1, STEPS) for m in range(lanes)
            ]
            piece = jnp.where(here.y * CORES + core == t, send(cuts[t], pairs), piece)
        got = [
            send(
                piece,
                [
                    (device(t, c, k, m), device(t, c, (k + d) % planes, m))
                    for k in range(1, STEPS) for t in range(n_y) for c in range(CORES) for m in range(lanes)
                ],
            )
            for d in range(1, planes)
        ]
        three = []
        for k in range(1, STEPS):
            value = piece
            for d in range(1, planes):
                value = jnp.where(plane == (k + d) % planes, got[d - 1], value)
            three.append(value)
        whole = plane_gather(jnp.concatenate(three, axis=0))
        other = core_exchange(whole)
        terms = [
            (
                k,
                gathered_pieces(
                    whole, other, (k - 1) * cut, cut, (STEPS - 1) * cut, lambda y, c, m: m * n_row + y * CORES + c
                ),
            )
            for k in range(1, STEPS)
        ]
        (out,) = run(current, terms, [(jnp.float32, 0, rows_here, True)])
        return out

    return on_device


def solution(mesh):
    placed = (P(AXES, None), P(AXES, None))
    on_device = make_on_device(mesh.shape["row"], mesh.shape["col"])
    return jax.shard_map(
        on_device, mesh=mesh, in_specs=placed, out_specs=P(AXES, None), check_vma=False
    )
```

```python
import functools

import jax
import jax.numpy as jnp
from jax import lax
from jax.experimental import pallas as pl
from jax.experimental.pallas import tpu as pltpu
from jax.sharding import PartitionSpec as P

NB = 2048
STEPS = 4
AXES = ("row", "col")
CORES = 2
TILE = 256
IN_FLIGHT = 3
MIB = 1024 * 1024


def after(value, *others):
    return lax.optimization_barrier((value, *others))[0]


class Place:
    def __init__(self, n_col, lanes):
        row, col = lax.axis_index("row"), lax.axis_index("col")
        self.y, self.core = row // CORES, row % CORES
        self.plane, self.lane = col // lanes, col % lanes
        self.block = (row * n_col + col) // lanes


def step_kernel(terms, handed, n_arrays, outs, where_am_i, only, *refs):
    refs = list(refs)
    current = refs.pop(0)
    panels = refs.pop(0) if any(near is None for _, _, near in terms) else None
    near_panels = [None if near is None else refs.pop(0) for _, _, near in terms]
    arrays, refs = refs[:n_arrays], refs[n_arrays:]
    results, refs = refs[: len(outs)], refs[len(outs) :]
    current_here, panels_here, held, sems, piece_sems, out_sems = refs
    rows = current.shape[0]
    tile = min(TILE, rows)
    here = where_am_i()

    def work():
        copies = [[] for _ in terms]
        for t, (_, pieces, _) in enumerate(terms):
            for array, first, size, place in pieces:
                start = pl.multiple_of(place(here) * size, size)
                copies[t].append(
                    pltpu.make_async_copy(
                        arrays[array].at[pl.ds(first, size), :],
                        held.at[t, pl.ds(start, size), :],
                        piece_sems.at[sum(len(c) for c in copies)],
                    )
                )

        def panel_copy(t, i):
            k = terms[t][0]
            return pltpu.make_async_copy(
                panels.at[pl.ds(i * tile, tile), pl.ds(k * NB, NB)], panels_here.at[t, i], sems.at[t, i]
            )

        def current_copy(i):
            at = pl.ds(i * tile, tile)
            return pltpu.make_async_copy(current.at[at, :], current_here.at[at, :], sems.at[len(terms), i])

        def load(t, i):
            if i == 0:
                for copy in copies[t]:
                    copy.start()
            if near_panels[t] is None:
                panel_copy(t, i).start()
            if t == 0:
                current_copy(i).start()

        order = [(t, i) for i in range(rows // tile) for t in range(len(terms))]
        in_flight = max(IN_FLIGHT, len(terms))
        for t, i in order[:in_flight]:
            load(t, i)
        sent = []
        for n, (t, i) in enumerate(order):
            at = pl.ds(i * tile, tile)
            if i == 0:
                for copy in copies[t]:
                    copy.wait()
            if t == 0:
                current_copy(i).wait()
                value = current_here[at, :]
            if near_panels[t] is None:
                panel_copy(t, i).wait()
                panel = panels_here[t, i]
            else:
                panel = near_panels[t][at, :]
            if n + in_flight < len(order):
                load(*order[n + in_flight])
            product = jnp.dot(panel, held[t], preferred_element_type=jnp.float32)
            value = jnp.where(here.block == terms[t][0], product, value - product)
            if t < len(terms) - 1:
                continue
            for o, (dtype, first, size, far) in enumerate(outs):
                low, high = max(first, i * tile), min(first + size, (i + 1) * tile)
                if low < high:
                    part = value[low - i * tile : high - i * tile].astype(dtype)
                    if far:
                        current_here[at, :] = part
                        sent.append(pltpu.make_async_copy(current_here.at[at, :], results[o].at[at, :], out_sems.at[i]))
                        sent[-1].start()
                    else:
                        results[o][pl.ds(low - first, high - low), :] = part
        for out in sent:
            out.wait()

    if only is None:
        work()
    else:
        pl.when(here.block == only)(work)
    for block, array in handed:

        def hand(array=array):
            copies = [
                pltpu.make_async_copy(arrays[array].at[pl.ds(first, size), :], results[o], piece_sems.at[o])
                for o, (_, first, size, _) in enumerate(outs)
            ]
            for copy in copies:
                copy.start()
            for copy in copies:
                copy.wait()

        pl.when(here.block == block)(hand)


def steps(current, factor_panels, terms, outs, where_am_i, only=None, handed=()):
    rows, scenarios = current.shape
    arrays = []

    def index(array):
        for i, other in enumerate(arrays):
            if other is array:
                return i
        arrays.append(array)
        return len(arrays) - 1

    plan = tuple(
        (k, tuple((index(array), first, size, place) for array, first, size, place in pieces), None if near is None else 0)
        for k, pieces, near in terms
    )
    near_panels = [near for _, _, near in terms if near is not None]
    handed = tuple((block, index(array)) for block, array in handed)
    n_terms = len(terms)
    tile = min(TILE, rows)
    n_pieces = max(sum(len(pieces) for _, pieces, _ in terms), len(outs))
    n_far = max(n_terms - len(near_panels), 1)
    assert not near_panels or len(near_panels) == n_terms
    anywhere = pl.BlockSpec(memory_space=pl.ANY)
    return pl.pallas_call(
        functools.partial(step_kernel, plan, handed, len(arrays), tuple(outs), where_am_i, only),
        in_specs=[anywhere] * (1 if near_panels else 2)
        + [pl.BlockSpec(memory_space=pltpu.VMEM)] * len(near_panels)
        + [anywhere] * len(arrays),
        out_specs=[anywhere if out[3] else pl.BlockSpec(memory_space=pltpu.VMEM) for out in outs],
        out_shape=[jax.ShapeDtypeStruct((size, scenarios), dtype) for dtype, _, size, _ in outs],
        scratch_shapes=[
            pltpu.VMEM((rows, scenarios), jnp.float32),
            pltpu.VMEM((n_far, 1 if near_panels else rows // tile, 16 if near_panels else tile, NB), jnp.bfloat16),
            pltpu.VMEM((n_terms, NB, scenarios), jnp.bfloat16),
            pltpu.SemaphoreType.DMA((n_terms + 1, rows // tile)),
            pltpu.SemaphoreType.DMA((n_pieces,)),
            pltpu.SemaphoreType.DMA((rows // tile,)),
        ],
        compiler_params=pltpu.CompilerParams(vmem_limit_bytes=(28 if near_panels else 48) * MIB),
        cost_estimate=pl.CostEstimate(
            flops=2 * rows * NB * scenarios * n_terms,
            bytes_accessed=8 * rows * scenarios,
            transcendentals=0,
        ),
    )(current, *([] if near_panels else [factor_panels]), *near_panels, *arrays)


def near_kernel(k, panels, out, sems):
    parts = sems.shape[0]
    rows = out.shape[0] // parts
    copies = []
    for i in range(parts):
        at = pl.ds(i * rows, rows)
        copies.append(pltpu.make_async_copy(panels.at[at, pl.ds(k * NB, NB)], out.at[at, :], sems.at[i]))
        copies[-1].start()
    for copy in copies:
        copy.wait()


def near_panel(factor_panels, k):
    rows = factor_panels.shape[0]
    return pl.pallas_call(
        functools.partial(near_kernel, k),
        in_specs=[pl.BlockSpec(memory_space=pl.ANY)],
        out_specs=pl.BlockSpec(memory_space=pl.ANY),
        out_shape=pltpu.VMEM((rows, NB), jnp.bfloat16),
        scratch_shapes=[pltpu.SemaphoreType.DMA((4,))],
        compiler_params=pltpu.CompilerParams(vmem_limit_bytes=44 * MIB),
        cost_estimate=pl.CostEstimate(flops=0, bytes_accessed=1, transcendentals=0),
    )(factor_panels)


def make_on_device(n_row, n_col):
    def on_device(rhs_scen, factor_panels):
        rows_here = factor_panels.shape[0]
        lanes = NB // rows_here
        planes = n_col // lanes
        n_y = n_row // CORES
        members = n_row * lanes
        where_am_i = functools.partial(Place, n_col, lanes)
        here = where_am_i()
        core, plane = here.core, here.plane

        def device(y, core, plane, lane):
            return (y * CORES + core) * n_col + plane * lanes + lane

        def send(value, pairs):
            return lax.ppermute(value, AXES, pairs)

        def run(current, terms, outs, only=None, handed=()):
            return steps(current, factor_panels, terms, outs, where_am_i, only, handed)

        def ahead(own, k):
            return [
                send(own, [(device(0, 0, k, (m + d) % lanes), device(0, 0, k + 1, m)) for m in range(lanes)])
                for d in range(lanes)
            ]

        along_x = [(0, d) for d in range(1, lanes)]
        along_y = [(d, 0) for d in range(1, n_y)]
        first_0, first_1 = along_x + along_y, along_y + along_x
        across = [(dy, dm) for dy, _ in along_y for _, dm in along_x]
        offsets = [((0, 0), (0, 0)), *zip(first_0, first_1), *zip(across, across)]

        def plane_gather(value):
            def pairs(c, step):
                return [
                    (device((t + step[0]) % n_y, c, z, (m + step[1]) % lanes), device(t, c, z, m))
                    for t in range(n_y) for z in range(planes) for m in range(lanes)
                ]

            got = [send(value, pairs(0, a) + pairs(1, b)) for a, b in zip(first_0, first_1)]
            last = []
            for dy, dm in across:
                a, b = first_0.index((dy, 0)), first_1.index((0, dm))
                payload = got[a] if a == b else jnp.where(core == 0, got[a], got[b])
                last.append(send(payload, pairs(0, (0, dm)) + pairs(1, (dy, 0))))
            return jnp.concatenate([value, *got, *last], axis=0)

        def core_exchange(value):
            pairs = [
                (device(t, 1 - c, z, m), device(t, c, z, m))
                for t in range(n_y) for c in range(CORES) for z in range(planes) for m in range(lanes)
            ]
            return send(value, pairs)

        def gathered_pieces(mine, other, first, size, stride, number):
            def place(offset, own, at):
                c = at.core if own else 1 - at.core
                a, b = (number((at.y + dy) % n_y, c, (at.lane + dm) % lanes) for dy, dm in offset)
                return a if offset[0] == offset[1] else jnp.where(c == 0, a, b)

            return [
                (array, i * stride + first, size, functools.partial(place, offset, array is mine))
                for array in (mine, other) for i, offset in enumerate(offsets)
            ]

        def lane_pieces(parts):
            return [
                (part, 0, rows_here, functools.partial(lambda d, at: (at.lane + d) % lanes, d))
                for d, part in enumerate(parts)
            ]

        f32_rows = (jnp.float32, 0, rows_here, False)
        own_rows = (jnp.bfloat16, 0, rows_here, False)
        cut = rows_here // n_row
        own_cuts = [(jnp.bfloat16, t * cut, cut, False) for t in range(n_row)]

        extra = NB // members
        first = rhs_scen[:, :NB].reshape(-1, n_row, 1, lanes, extra)
        first = jnp.broadcast_to(first, (first.shape[0], n_row, planes, lanes, extra))
        first = first.reshape(first.shape[0], n_row * n_col, extra)
        outgoing = jnp.concatenate(
            [rhs_scen.reshape(rhs_scen.shape[0], n_row * n_col, rows_here), first], axis=2
        )
        regrouped = lax.all_to_all(outgoing, AXES, split_axis=1, concat_axis=0, tiled=True)
        regrouped = regrouped.reshape(-1, rows_here + extra)
        current = jnp.transpose(regrouped[:, :rows_here]).astype(jnp.float32)
        whole = plane_gather(jnp.transpose(regrouped[:, rows_here:]))
        pieces = gathered_pieces(
            whole, core_exchange(whole), 0, extra, extra, lambda y, c, m: (y * CORES + c) * lanes + m
        )
        current, own1 = run(current, [(0, pieces, None)], [f32_rows, own_rows])

        hop1 = ahead(own1, 1)
        near1 = near_panel(after(factor_panels, own1), 1)
        start1 = after(own1, hop1[0], near1)
        at_3 = [
            send(start1, [(device(0, 0, 1, (m + d) % lanes), device(0, 0, 3, m)) for m in range(lanes)])
            for d in range(lanes)
        ]
        (own2,) = run(current, [(1, lane_pieces(hop1), near1)], [own_rows], 2)
        hop2 = ahead(own2, 2)
        near2 = near_panel(after(factor_panels, own2), 2)
        (chained,) = run(after(current, near2), [(1, lane_pieces(at_3), near1)], [f32_rows], 3)
        cuts = run(chained, [(2, lane_pieces(hop2), near2)], own_cuts, 3, [(1, own1), (2, own2)])

        piece = cuts[0]
        for t in range(1, n_row):
            pairs = [
                (device(0, 0, k, m), device(t // CORES, t % CORES, k, m)) for k in range(1, STEPS) for m in range(lanes)
            ]
            piece = jnp.where(here.y * CORES + core == t, send(cuts[t], pairs), piece)
        got = [
            send(
                piece,
                [
                    (device(t, c, k, m), device(t, c, (k + d) % planes, m))
                    for k in range(1, STEPS) for t in range(n_y) for c in range(CORES) for m in range(lanes)
                ],
            )
            for d in range(1, planes)
        ]
        three = []
        for k in range(1, STEPS):
            value = piece
            for d in range(1, planes):
                value = jnp.where(plane == (k + d) % planes, got[d - 1], value)
            three.append(value)
        near3 = near_panel(after(factor_panels, cuts[0]), 3)
        whole = plane_gather(after(jnp.concatenate(three, axis=0), near3))
        other = core_exchange(whole)
        terms = [
            (
                k,
                gathered_pieces(
                    whole, other, (k - 1) * cut, cut, (STEPS - 1) * cut, lambda y, c, m: m * n_row + y * CORES + c
                ),
                near,
            )
            for k, near in ((1, near1), (2, near2), (3, near3))
        ]
        (out,) = run(current, terms, [(jnp.float32, 0, rows_here, True)])
        return out

    return on_device


def solution(mesh):
    placed = (P(AXES, None), P(AXES, None))
    on_device = make_on_device(mesh.shape["row"], mesh.shape["col"])
    return jax.shard_map(
        on_device, mesh=mesh, in_specs=placed, out_specs=P(AXES, None), check_vma=False
    )
```

```python
import functools

import jax
import jax.numpy as jnp
from jax import lax
from jax.experimental import pallas as pl
from jax.experimental.pallas import tpu as pltpu
from jax.sharding import PartitionSpec as P

NB = 2048
STEPS = 4
AXES = ("row", "col")
CORES = 2
TILE = 256
NEAR_TILE = 512
IN_FLIGHT = 3
MIB = 1024 * 1024


def after(value, *others):
    return lax.optimization_barrier((value, *others))[0]


class Place:
    def __init__(self, n_col, lanes):
        row, col = lax.axis_index("row"), lax.axis_index("col")
        self.y, self.core = row // CORES, row % CORES
        self.plane, self.lane = col // lanes, col % lanes
        self.block = (row * n_col + col) // lanes


def step_kernel(terms, handed, n_arrays, outs, where_am_i, only, *refs):
    refs = list(refs)
    current = refs.pop(0)
    panels = refs.pop(0) if any(near is None for _, _, near, _ in terms) else None
    near_panels = [None if near is None else refs.pop(0) for _, _, near, _ in terms]
    arrays, refs = refs[:n_arrays], refs[n_arrays:]
    results, refs = refs[: len(outs)], refs[len(outs) :]
    current_here, panels_here, held, sems, piece_sems, out_sems = refs
    rows = current.shape[0]
    tile = min(NEAR_TILE if near_panels[0] is not None else TILE, rows)
    here = where_am_i()

    def work():
        copies = [[] for _ in terms]
        places, part_of_block = [], []
        for t, (_, pieces, _, _) in enumerate(terms):
            places.append([pl.multiple_of(place(here) * size, size) for _, _, size, place in pieces])
            part_of_block.append(sum(size for _, _, size, _ in pieces) < NB)
            for j, (array, first, size, _) in enumerate(pieces):
                start = j * size if part_of_block[t] else places[t][j]
                copies[t].append(
                    pltpu.make_async_copy(
                        arrays[array].at[pl.ds(first, size), :],
                        held.at[t, pl.ds(start, size), :],
                        piece_sems.at[sum(len(c) for c in copies)],
                    )
                )

        def panel_copy(t, i):
            k = terms[t][0]
            return pltpu.make_async_copy(
                panels.at[pl.ds(i * tile, tile), pl.ds(k * NB, NB)], panels_here.at[t, i], sems.at[t, i]
            )

        def current_copy(i):
            at = pl.ds(i * tile, tile)
            return pltpu.make_async_copy(current.at[at, :], current_here.at[at, :], sems.at[len(terms), i])

        def load(t, i):
            if i == 0:
                for copy in copies[t]:
                    copy.start()
            if near_panels[t] is None:
                panel_copy(t, i).start()
            if t == 0:
                current_copy(i).start()

        order = [(t, i) for i in range(rows // tile) for t in range(len(terms))]
        in_flight = max(IN_FLIGHT, len(terms))
        for t, i in order[:in_flight]:
            load(t, i)
        sent = []
        for n, (t, i) in enumerate(order):
            at = pl.ds(i * tile, tile)
            if i == 0:
                for copy in copies[t]:
                    copy.wait()
            if t == 0:
                current_copy(i).wait()
                value = current_here[at, :]
            if near_panels[t] is None:
                panel_copy(t, i).wait()
                panel = panels_here[t, i]
            else:
                if part_of_block[t]:
                    sizes = [size for _, _, size, _ in terms[t][1]]
                    panel = jnp.concatenate(
                        [near_panels[t][at, pl.ds(start, size)] for start, size in zip(places[t], sizes)], axis=1
                    )
                else:
                    panel = near_panels[t][at, :]
            if n + in_flight < len(order):
                load(*order[n + in_flight])
            product = jnp.dot(panel, held[t, : panel.shape[1]], preferred_element_type=jnp.float32)
            k, fresh = terms[t][0], terms[t][3]
            less = value - product
            if not fresh:
                less = jnp.where((here.block > k) & (here.block < STEPS), value, less)
            value = jnp.where(here.block == k, product if fresh else value + product, less)
            if t < len(terms) - 1:
                continue
            for o, (dtype, first, size, far) in enumerate(outs):
                low, high = max(first, i * tile), min(first + size, (i + 1) * tile)
                if low < high:
                    part = value[low - i * tile : high - i * tile].astype(dtype)
                    if far:
                        current_here[at, :] = part
                        sent.append(pltpu.make_async_copy(current_here.at[at, :], results[o].at[at, :], out_sems.at[i]))
                        sent[-1].start()
                    else:
                        results[o][pl.ds(low - first, high - low), :] = part
        for out in sent:
            out.wait()

    if only is None:
        work()
    else:
        pl.when(here.block == only)(work)
    for block, array in handed:

        def hand(array=array):
            copies = [
                pltpu.make_async_copy(arrays[array].at[pl.ds(first, size), :], results[o], piece_sems.at[o])
                for o, (_, first, size, _) in enumerate(outs)
            ]
            for copy in copies:
                copy.start()
            for copy in copies:
                copy.wait()

        pl.when(here.block == block)(hand)


def steps(current, factor_panels, terms, outs, where_am_i, only=None, handed=()):
    rows, scenarios = current.shape
    arrays = []

    def index(array):
        for i, other in enumerate(arrays):
            if other is array:
                return i
        arrays.append(array)
        return len(arrays) - 1

    plan = tuple(
        (k, tuple((index(array), first, size, place) for array, first, size, place in pieces), None if near is None else 0, fresh)
        for k, pieces, near, fresh in terms
    )
    near_panels = [near for _, _, near, _ in terms if near is not None]
    handed = tuple((block, index(array)) for block, array in handed)
    n_terms = len(terms)
    tile = min(NEAR_TILE if near_panels else TILE, rows)
    n_pieces = max(sum(len(pieces) for _, pieces, _, _ in terms), len(outs))
    n_far = max(n_terms - len(near_panels), 1)
    assert not near_panels or len(near_panels) == n_terms
    anywhere = pl.BlockSpec(memory_space=pl.ANY)
    return pl.pallas_call(
        functools.partial(step_kernel, plan, handed, len(arrays), tuple(outs), where_am_i, only),
        in_specs=[anywhere] * (1 if near_panels else 2)
        + [pl.BlockSpec(memory_space=pltpu.VMEM)] * len(near_panels)
        + [anywhere] * len(arrays),
        out_specs=[anywhere if out[3] else pl.BlockSpec(memory_space=pltpu.VMEM) for out in outs],
        out_shape=[jax.ShapeDtypeStruct((size, scenarios), dtype) for dtype, _, size, _ in outs],
        scratch_shapes=[
            pltpu.VMEM((rows, scenarios), jnp.float32),
            pltpu.VMEM((n_far, 1 if near_panels else rows // tile, 16 if near_panels else tile, NB), jnp.bfloat16),
            pltpu.VMEM((n_terms, NB, scenarios), jnp.bfloat16),
            pltpu.SemaphoreType.DMA((n_terms + 1, rows // tile)),
            pltpu.SemaphoreType.DMA((n_pieces,)),
            pltpu.SemaphoreType.DMA((rows // tile,)),
        ],
        compiler_params=pltpu.CompilerParams(vmem_limit_bytes=(28 if near_panels else 48) * MIB),
        cost_estimate=pl.CostEstimate(
            flops=2 * rows * NB * scenarios * n_terms,
            bytes_accessed=8 * rows * scenarios,
            transcendentals=0,
        ),
    )(current, *([] if near_panels else [factor_panels]), *near_panels, *arrays)


def near_kernel(k, panels, out, sems):
    parts = sems.shape[0]
    rows = out.shape[0] // parts
    copies = []
    for i in range(parts):
        at = pl.ds(i * rows, rows)
        copies.append(pltpu.make_async_copy(panels.at[at, pl.ds(k * NB, NB)], out.at[at, :], sems.at[i]))
        copies[-1].start()
    for copy in copies:
        copy.wait()


def near_panel(factor_panels, k):
    rows = factor_panels.shape[0]
    return pl.pallas_call(
        functools.partial(near_kernel, k),
        in_specs=[pl.BlockSpec(memory_space=pl.ANY)],
        out_specs=pl.BlockSpec(memory_space=pl.ANY),
        out_shape=pltpu.VMEM((rows, NB), jnp.bfloat16),
        scratch_shapes=[pltpu.SemaphoreType.DMA((4,))],
        compiler_params=pltpu.CompilerParams(vmem_limit_bytes=44 * MIB),
        cost_estimate=pl.CostEstimate(flops=0, bytes_accessed=1, transcendentals=0),
    )(factor_panels)


def make_on_device(n_row, n_col):
    def on_device(rhs_scen, factor_panels):
        rows_here = factor_panels.shape[0]
        lanes = NB // rows_here
        planes = n_col // lanes
        n_y = n_row // CORES
        members = n_row * lanes
        where_am_i = functools.partial(Place, n_col, lanes)
        here = where_am_i()
        core, plane = here.core, here.plane

        def device(y, core, plane, lane):
            return (y * CORES + core) * n_col + plane * lanes + lane

        def send(value, pairs):
            return lax.ppermute(value, AXES, pairs)

        def run(current, terms, outs, only=None, handed=()):
            return steps(current, factor_panels, terms, outs, where_am_i, only, handed)

        def ahead(own, k):
            return [
                send(own, [(device(0, 0, k, (m + d) % lanes), device(0, 0, k + 1, m)) for m in range(lanes)])
                for d in range(lanes)
            ]

        along_x = [(0, d) for d in range(1, lanes)]
        along_y = [(d, 0) for d in range(1, n_y)]
        first_0, first_1 = along_x + along_y, along_y + along_x
        across = [(dy, dm) for dy, _ in along_y for _, dm in along_x]
        offsets = [((0, 0), (0, 0)), *zip(first_0, first_1), *zip(across, across)]

        def plane_gather(value):
            def pairs(c, step):
                return [
                    (device((t + step[0]) % n_y, c, z, (m + step[1]) % lanes), device(t, c, z, m))
                    for t in range(n_y) for z in range(planes) for m in range(lanes)
                ]

            got = [send(value, pairs(0, a) + pairs(1, b)) for a, b in zip(first_0, first_1)]
            last = []
            for dy, dm in across:
                a, b = first_0.index((dy, 0)), first_1.index((0, dm))
                payload = got[a] if a == b else jnp.where(core == 0, got[a], got[b])
                last.append(send(payload, pairs(0, (0, dm)) + pairs(1, (dy, 0))))
            return jnp.concatenate([value, *got], axis=0), jnp.concatenate(last, axis=0)

        def core_exchange(value):
            pairs = [
                (device(t, 1 - c, z, m), device(t, c, z, m))
                for t in range(n_y) for c in range(CORES) for z in range(planes) for m in range(lanes)
            ]
            return send(value, pairs)

        def gathered_pieces(array, own, first, size, stride, offsets, number):
            def place(offset, own, at):
                c = at.core if own else 1 - at.core
                a, b = (number((at.y + dy) % n_y, c, (at.lane + dm) % lanes) for dy, dm in offset)
                return a if offset[0] == offset[1] else jnp.where(c == 0, a, b)

            return [
                (array, i * stride + first, size, functools.partial(place, offset, own))
                for i, offset in enumerate(offsets)
            ]

        def lane_pieces(parts):
            return [
                (part, 0, rows_here, functools.partial(lambda d, at: (at.lane + d) % lanes, d))
                for d, part in enumerate(parts)
            ]

        f32_rows = (jnp.float32, 0, rows_here, False)
        own_rows = (jnp.bfloat16, 0, rows_here, False)
        cut = rows_here // n_row
        own_cuts = [(jnp.bfloat16, t * cut, cut, False) for t in range(n_row)]

        extra = NB // members
        first = rhs_scen[:, :NB].reshape(-1, n_row, 1, lanes, extra)
        first = jnp.broadcast_to(first, (first.shape[0], n_row, planes, lanes, extra))
        first = first.reshape(first.shape[0], n_row * n_col, extra)
        outgoing = jnp.concatenate(
            [rhs_scen.reshape(rhs_scen.shape[0], n_row * n_col, rows_here), first], axis=2
        )
        regrouped = lax.all_to_all(outgoing, AXES, split_axis=1, concat_axis=0, tiled=True)
        regrouped = regrouped.reshape(-1, rows_here + extra)
        current = jnp.transpose(regrouped[:, :rows_here]).astype(jnp.float32)
        whole = jnp.concatenate(plane_gather(jnp.transpose(regrouped[:, rows_here:])), axis=0)
        pieces = [
            piece
            for array, own in ((whole, True), (core_exchange(whole), False))
            for piece in gathered_pieces(
                array, own, 0, extra, extra, offsets, lambda y, c, m: (y * CORES + c) * lanes + m
            )
        ]
        current, own1 = run(current, [(0, pieces, None, True)], [f32_rows, own_rows])

        hop1 = ahead(own1, 1)
        near1 = near_panel(after(factor_panels, own1), 1)
        near2 = near_panel(after(factor_panels, own1), 2)
        start1 = after(own1, hop1[0], near1, near2)
        to_3 = send(start1, [(device(0, 0, 1, m), device(0, 0, 3, m)) for m in range(lanes)])
        (own2,) = run(current, [(1, lane_pieces(hop1), near1, True)], [own_rows], 2)
        hop2 = ahead(own2, 2)
        to_3 = after(to_3, own2)
        at_3 = [to_3] + [
            send(to_3, [(device(0, 0, 3, (m + d) % lanes), device(0, 0, 3, m)) for m in range(lanes)])
            for d in range(1, lanes)
        ]
        (chained,) = run(current, [(1, lane_pieces(at_3), near1, True)], [f32_rows], 3)
        cuts = run(chained, [(2, lane_pieces(hop2), near2, True)], own_cuts, 3, [(1, own1), (2, own2)])

        piece = cuts[0]
        for t in range(1, n_row):
            pairs = [
                (device(0, 0, k, m), device(t // CORES, t % CORES, k, m)) for k in range(1, STEPS) for m in range(lanes)
            ]
            piece = jnp.where(here.y * CORES + core == t, send(cuts[t], pairs), piece)
        got = [
            send(
                piece,
                [
                    (device(t, c, k, m), device(t, c, (k + d) % planes, m))
                    for k in range(1, STEPS) for t in range(n_y) for c in range(CORES) for m in range(lanes)
                ],
            )
            for d in range(1, planes)
        ]
        three = []
        for k in range(1, STEPS):
            value = piece
            for d in range(1, planes):
                value = jnp.where(plane == (k + d) % planes, got[d - 1], value)
            three.append(value)
        near3 = near_panel(after(factor_panels, cuts[0]), 3)
        most, last = plane_gather(after(jnp.concatenate(three, axis=0), near3))
        n_most = len(offsets) - len(across)

        def terms(fresh, *arrays):
            return [
                (
                    k,
                    [
                        piece
                        for array, own, start, count in arrays
                        for piece in gathered_pieces(
                            array, own, (k - 1) * cut, cut, (STEPS - 1) * cut, offsets[start : start + count],
                            lambda y, c, m: m * n_row + y * CORES + c,
                        )
                    ],
                    near,
                    fresh,
                )
                for k, near in ((1, near1), (2, near2), (3, near3))
            ]

        (current,) = run(current, terms(True, (most, True, 0, n_most)), [f32_rows])
        whole = after(jnp.concatenate([most, last], axis=0), current)
        other = core_exchange(whole)
        rest = [(last, True, n_most, len(across)), (other, False, 0, len(offsets))]
        (out,) = run(current, terms(False, *rest), [(jnp.float32, 0, rows_here, True)])
        return out

    return on_device


def solution(mesh):
    placed = (P(AXES, None), P(AXES, None))
    on_device = make_on_device(mesh.shape["row"], mesh.shape["col"])
    return jax.shard_map(
        on_device, mesh=mesh, in_specs=placed, out_specs=P(AXES, None), check_vma=False
    )
```

```python
import functools

import jax
import jax.numpy as jnp
from jax import lax
from jax.experimental import pallas as pl
from jax.experimental.pallas import tpu as pltpu
from jax.sharding import PartitionSpec as P

NB = 2048
STEPS = 4
AXES = ("row", "col")
CORES = 2
TILE = 256
NEAR_TILE = 512
IN_FLIGHT = 3
MIB = 1024 * 1024


def after(value, *others):
    return lax.optimization_barrier((value, *others))[0]


class Place:
    def __init__(self, n_col, lanes):
        row, col = lax.axis_index("row"), lax.axis_index("col")
        self.y, self.core = row // CORES, row % CORES
        self.plane, self.lane = col // lanes, col % lanes
        self.block = (row * n_col + col) // lanes


def step_kernel(terms, handed, n_arrays, outs, where_am_i, only, *refs):
    refs = list(refs)
    current = refs.pop(0)
    panels = refs.pop(0) if any(near is None for _, _, near, _ in terms) else None
    near_panels = [None if near is None else refs.pop(0) for _, _, near, _ in terms]
    arrays, refs = refs[:n_arrays], refs[n_arrays:]
    results, refs = refs[: len(outs)], refs[len(outs) :]
    current_here, panels_here, held, sems, piece_sems, out_sems = refs
    rows = current.shape[0]
    tile = min(NEAR_TILE if near_panels[0] is not None else TILE, rows)
    here = where_am_i()

    def work():
        copies = [[] for _ in terms]
        places, part_of_block = [], []
        for t, (_, pieces, _, _) in enumerate(terms):
            places.append([pl.multiple_of(place(here) * size, size) for _, _, size, place in pieces])
            part_of_block.append(sum(size for _, _, size, _ in pieces) < NB)
            for j, (array, first, size, _) in enumerate(pieces):
                start = j * size if part_of_block[t] else places[t][j]
                copies[t].append(
                    pltpu.make_async_copy(
                        arrays[array].at[pl.ds(first, size), :],
                        held.at[t, pl.ds(start, size), :],
                        piece_sems.at[sum(len(c) for c in copies)],
                    )
                )

        def panel_copy(t, i):
            k = terms[t][0]
            return pltpu.make_async_copy(
                panels.at[pl.ds(i * tile, tile), pl.ds(k * NB, NB)], panels_here.at[t, i], sems.at[t, i]
            )

        def current_copy(i):
            at = pl.ds(i * tile, tile)
            return pltpu.make_async_copy(current.at[at, :], current_here.at[at, :], sems.at[len(terms), i])

        def load(t, i):
            if i == 0:
                for copy in copies[t]:
                    copy.start()
            if near_panels[t] is None:
                panel_copy(t, i).start()
            if t == 0:
                current_copy(i).start()

        order = [(t, i) for i in range(rows // tile) for t in range(len(terms))]
        in_flight = max(IN_FLIGHT, len(terms))
        for t, i in order[:in_flight]:
            load(t, i)
        sent = []
        for n, (t, i) in enumerate(order):
            at = pl.ds(i * tile, tile)
            if i == 0:
                for copy in copies[t]:
                    copy.wait()
            if t == 0:
                current_copy(i).wait()
                value = current_here[at, :]
            if near_panels[t] is None:
                panel_copy(t, i).wait()
                panel = panels_here[t, i]
            else:
                if part_of_block[t]:
                    sizes = [size for _, _, size, _ in terms[t][1]]
                    panel = jnp.concatenate(
                        [near_panels[t][at, pl.ds(start, size)] for start, size in zip(places[t], sizes)], axis=1
                    )
                else:
                    panel = near_panels[t][at, :]
            if n + in_flight < len(order):
                load(*order[n + in_flight])
            product = jnp.dot(panel, held[t, : panel.shape[1]], preferred_element_type=jnp.float32)
            k, fresh = terms[t][0], terms[t][3]
            less = value - product
            if not fresh:
                less = jnp.where((here.block > k) & (here.block < STEPS), value, less)
            value = jnp.where(here.block == k, product if fresh else value + product, less)
            if t < len(terms) - 1:
                continue
            for o, (dtype, first, size, far) in enumerate(outs):
                low, high = max(first, i * tile), min(first + size, (i + 1) * tile)
                if low < high:
                    part = value[low - i * tile : high - i * tile].astype(dtype)
                    if far:
                        current_here[at, :] = part
                        sent.append(pltpu.make_async_copy(current_here.at[at, :], results[o].at[at, :], out_sems.at[i]))
                        sent[-1].start()
                    else:
                        results[o][pl.ds(low - first, high - low), :] = part
        for out in sent:
            out.wait()

    if only is None:
        work()
    else:
        pl.when(here.block == only)(work)
    for block, array in handed:

        def hand(array=array):
            copies = [
                pltpu.make_async_copy(arrays[array].at[pl.ds(first, size), :], results[o], piece_sems.at[o])
                for o, (_, first, size, _) in enumerate(outs)
            ]
            for copy in copies:
                copy.start()
            for copy in copies:
                copy.wait()

        pl.when(here.block == block)(hand)


def steps(current, factor_panels, terms, outs, where_am_i, only=None, handed=()):
    rows, scenarios = current.shape
    arrays = []

    def index(array):
        for i, other in enumerate(arrays):
            if other is array:
                return i
        arrays.append(array)
        return len(arrays) - 1

    plan = tuple(
        (k, tuple((index(array), first, size, place) for array, first, size, place in pieces), None if near is None else 0, fresh)
        for k, pieces, near, fresh in terms
    )
    near_panels = [near for _, _, near, _ in terms if near is not None]
    handed = tuple((block, index(array)) for block, array in handed)
    n_terms = len(terms)
    tile = min(NEAR_TILE if near_panels else TILE, rows)
    n_pieces = max(sum(len(pieces) for _, pieces, _, _ in terms), len(outs))
    n_far = max(n_terms - len(near_panels), 1)
    assert not near_panels or len(near_panels) == n_terms
    anywhere = pl.BlockSpec(memory_space=pl.ANY)
    return pl.pallas_call(
        functools.partial(step_kernel, plan, handed, len(arrays), tuple(outs), where_am_i, only),
        in_specs=[anywhere] * (1 if near_panels else 2)
        + [pl.BlockSpec(memory_space=pltpu.VMEM)] * len(near_panels)
        + [anywhere] * len(arrays),
        out_specs=[anywhere if out[3] else pl.BlockSpec(memory_space=pltpu.VMEM) for out in outs],
        out_shape=[jax.ShapeDtypeStruct((size, scenarios), dtype) for dtype, _, size, _ in outs],
        scratch_shapes=[
            pltpu.VMEM((rows, scenarios), jnp.float32),
            pltpu.VMEM((n_far, 1 if near_panels else rows // tile, 16 if near_panels else tile, NB), jnp.bfloat16),
            pltpu.VMEM((n_terms, NB, scenarios), jnp.bfloat16),
            pltpu.SemaphoreType.DMA((n_terms + 1, rows // tile)),
            pltpu.SemaphoreType.DMA((n_pieces,)),
            pltpu.SemaphoreType.DMA((rows // tile,)),
        ],
        compiler_params=pltpu.CompilerParams(vmem_limit_bytes=(28 if near_panels else 48) * MIB),
        cost_estimate=pl.CostEstimate(
            flops=2 * rows * NB * scenarios * n_terms,
            bytes_accessed=8 * rows * scenarios,
            transcendentals=0,
        ),
    )(current, *([] if near_panels else [factor_panels]), *near_panels, *arrays)


def near_kernel(k, panels, out, sems):
    parts = sems.shape[0]
    rows = out.shape[0] // parts
    copies = []
    for i in range(parts):
        at = pl.ds(i * rows, rows)
        copies.append(pltpu.make_async_copy(panels.at[at, pl.ds(k * NB, NB)], out.at[at, :], sems.at[i]))
        copies[-1].start()
    for copy in copies:
        copy.wait()


def near_panel(factor_panels, k):
    rows = factor_panels.shape[0]
    return pl.pallas_call(
        functools.partial(near_kernel, k),
        in_specs=[pl.BlockSpec(memory_space=pl.ANY)],
        out_specs=pl.BlockSpec(memory_space=pl.ANY),
        out_shape=pltpu.VMEM((rows, NB), jnp.bfloat16),
        scratch_shapes=[pltpu.SemaphoreType.DMA((4,))],
        compiler_params=pltpu.CompilerParams(vmem_limit_bytes=44 * MIB),
        cost_estimate=pl.CostEstimate(flops=0, bytes_accessed=1, transcendentals=0),
    )(factor_panels)


def make_on_device(n_row, n_col):
    def on_device(rhs_scen, factor_panels):
        rows_here = factor_panels.shape[0]
        lanes = NB // rows_here
        planes = n_col // lanes
        n_y = n_row // CORES
        members = n_row * lanes
        where_am_i = functools.partial(Place, n_col, lanes)
        here = where_am_i()
        core, plane = here.core, here.plane

        def device(y, core, plane, lane):
            return (y * CORES + core) * n_col + plane * lanes + lane

        def send(value, pairs):
            return lax.ppermute(value, AXES, pairs)

        def run(current, terms, outs, only=None, handed=()):
            return steps(current, factor_panels, terms, outs, where_am_i, only, handed)

        def ahead(own, k):
            return [
                send(own, [(device(0, 0, k, (m + d) % lanes), device(0, 0, k + 1, m)) for m in range(lanes)])
                for d in range(lanes)
            ]

        along_x = [(0, d) for d in range(1, lanes)]
        along_y = [(d, 0) for d in range(1, n_y)]
        first_0, first_1 = along_x + along_y, along_y + along_x
        across = [(dy, dm) for dy, _ in along_y for _, dm in along_x]
        offsets = [((0, 0), (0, 0)), *zip(first_0, first_1), *zip(across, across)]

        def plane_gather(value, beside=None):
            def pairs(c, step):
                return [
                    (device((t + step[0]) % n_y, c, z, (m + step[1]) % lanes), device(t, c, z, m))
                    for t in range(n_y) for z in range(planes) for m in range(lanes)
                ]

            got = [send(value, pairs(0, a) + pairs(1, b)) for a, b in zip(first_0, first_1)]
            if beside is not None:
                got = [after(part, beside) for part in got]
            last = []
            for dy, dm in across:
                a, b = first_0.index((dy, 0)), first_1.index((0, dm))
                payload = got[a] if a == b else jnp.where(core == 0, got[a], got[b])
                last.append(send(payload, pairs(0, (0, dm)) + pairs(1, (dy, 0))))
            return jnp.concatenate([value, *got], axis=0), jnp.concatenate(last, axis=0)

        def core_exchange(value):
            pairs = [
                (device(t, 1 - c, z, m), device(t, c, z, m))
                for t in range(n_y) for c in range(CORES) for z in range(planes) for m in range(lanes)
            ]
            return send(value, pairs)

        def gathered_pieces(array, own, first, size, stride, offsets, number):
            def place(offset, own, at):
                c = at.core if own else 1 - at.core
                a, b = (number((at.y + dy) % n_y, c, (at.lane + dm) % lanes) for dy, dm in offset)
                return a if offset[0] == offset[1] else jnp.where(c == 0, a, b)

            return [
                (array, i * stride + first, size, functools.partial(place, offset, own))
                for i, offset in enumerate(offsets)
            ]

        def lane_pieces(parts):
            return [
                (part, 0, rows_here, functools.partial(lambda d, at: (at.lane + d) % lanes, d))
                for d, part in enumerate(parts)
            ]

        f32_rows = (jnp.float32, 0, rows_here, False)
        own_rows = (jnp.bfloat16, 0, rows_here, False)
        cut = rows_here // n_row
        own_cuts = [(jnp.bfloat16, t * cut, cut, False) for t in range(n_row)]

        extra = NB // members
        first = rhs_scen.reshape(rhs_scen.shape[0], -1, extra)[:, :members].reshape(-1, n_row, 1, lanes, extra)
        first = jnp.broadcast_to(first, (first.shape[0], n_row, planes, lanes, extra))
        first = first.reshape(first.shape[0], n_row * n_col, extra)
        outgoing = jnp.concatenate(
            [rhs_scen.reshape(rhs_scen.shape[0], n_row * n_col, rows_here), first], axis=2
        )
        regrouped = lax.all_to_all(outgoing, AXES, split_axis=1, concat_axis=0, tiled=True)
        regrouped = regrouped.reshape(-1, rows_here + extra)
        current = jnp.transpose(regrouped[:, :rows_here]).astype(jnp.float32)
        near0 = near_panel(after(factor_panels, regrouped), 0)
        whole = jnp.concatenate(plane_gather(jnp.transpose(regrouped[:, rows_here:]), near0), axis=0)
        pieces = [
            piece
            for array, own in ((whole, True), (core_exchange(whole), False))
            for piece in gathered_pieces(
                array, own, 0, extra, extra, offsets, lambda y, c, m: (y * CORES + c) * lanes + m
            )
        ]
        current, own1 = run(current, [(0, pieces, near0, True)], [f32_rows, own_rows])

        hop1 = ahead(own1, 1)
        near1 = near_panel(after(factor_panels, own1), 1)
        start1 = after(own1, hop1[0], near1)
        at_3 = [
            send(start1, [(device(0, 0, 1, (m + d) % lanes), device(0, 0, 3, m)) for m in range(lanes)])
            for d in range(lanes)
        ]
        (own2,) = run(current, [(1, lane_pieces(hop1), near1, True)], [own_rows], 2)
        hop2 = ahead(own2, 2)
        near2 = near_panel(after(factor_panels, own2), 2)
        (chained,) = run(after(current, near2), [(1, lane_pieces(at_3), near1, True)], [f32_rows], 3)
        cuts = run(chained, [(2, lane_pieces(hop2), near2, True)], own_cuts, 3, [(1, own1), (2, own2)])

        piece = cuts[0]
        for t in range(1, n_row):
            pairs = [
                (device(0, 0, k, m), device(t // CORES, t % CORES, k, m)) for k in range(1, STEPS) for m in range(lanes)
            ]
            piece = jnp.where(here.y * CORES + core == t, send(cuts[t], pairs), piece)
        got = [
            send(
                piece,
                [
                    (device(t, c, k, m), device(t, c, (k + d) % planes, m))
                    for k in range(1, STEPS) for t in range(n_y) for c in range(CORES) for m in range(lanes)
                ],
            )
            for d in range(1, planes)
        ]
        three = []
        for k in range(1, STEPS):
            value = piece
            for d in range(1, planes):
                value = jnp.where(plane == (k + d) % planes, got[d - 1], value)
            three.append(value)
        near3 = near_panel(after(factor_panels, cuts[0]), 3)
        most, last = plane_gather(after(jnp.concatenate(three, axis=0), near3))
        n_most = len(offsets) - len(across)

        def terms(fresh, *arrays):
            return [
                (
                    k,
                    [
                        piece
                        for array, own, start, count in arrays
                        for piece in gathered_pieces(
                            array, own, (k - 1) * cut, cut, (STEPS - 1) * cut, offsets[start : start + count],
                            lambda y, c, m: m * n_row + y * CORES + c,
                        )
                    ],
                    near,
                    fresh,
                )
                for k, near in ((1, near1), (2, near2), (3, near3))
            ]

        (current,) = run(current, terms(True, (most, True, 0, n_most)), [f32_rows])
        whole = after(jnp.concatenate([most, last], axis=0), current)
        other = core_exchange(whole)
        rest = [(last, True, n_most, len(across)), (other, False, 0, len(offsets))]
        (out,) = run(current, terms(False, *rest), [(jnp.float32, 0, rows_here, True)])
        return out

    return on_device


def solution(mesh):
    placed = (P(AXES, None), P(AXES, None))
    on_device = make_on_device(mesh.shape["row"], mesh.shape["col"])
    return jax.shard_map(
        on_device, mesh=mesh, in_specs=placed, out_specs=P(AXES, None), check_vma=False
    )
```

```python
import functools

import jax
import jax.numpy as jnp
from jax import lax
from jax.experimental import pallas as pl
from jax.experimental.pallas import tpu as pltpu
from jax.sharding import PartitionSpec as P

NB = 2048
STEPS = 4
AXES = ("row", "col")
CORES = 2
TILE = 256
NEAR_TILE = 512
IN_FLIGHT = 3
MIB = 1024 * 1024


def after(value, *others):
    return lax.optimization_barrier((value, *others))[0]


class Place:
    def __init__(self, n_col, lanes):
        row, col = lax.axis_index("row"), lax.axis_index("col")
        self.y, self.core = row // CORES, row % CORES
        self.plane, self.lane = col // lanes, col % lanes
        self.block = (row * n_col + col) // lanes


def step_kernel(terms, handed, n_arrays, outs, where_am_i, only, *refs):
    refs = list(refs)
    current = refs.pop(0)
    panels = refs.pop(0) if any(near is None for _, _, near, _ in terms) else None
    near_panels = [None if near is None else refs.pop(0) for _, _, near, _ in terms]
    arrays, refs = refs[:n_arrays], refs[n_arrays:]
    results, refs = refs[: len(outs)], refs[len(outs) :]
    current_here, panels_here, held, sems, piece_sems, out_sems = refs
    rows = current.shape[0]
    tile = min(NEAR_TILE if near_panels[0] is not None else TILE, rows)
    here = where_am_i()

    def work():
        copies = [[] for _ in terms]
        places, part_of_block = [], []
        for t, (_, pieces, _, _) in enumerate(terms):
            places.append([pl.multiple_of(place(here) * size, size) for _, _, size, place in pieces])
            part_of_block.append(sum(size for _, _, size, _ in pieces) < NB)
            for j, (array, first, size, _) in enumerate(pieces):
                start = j * size if part_of_block[t] else places[t][j]
                copies[t].append(
                    pltpu.make_async_copy(
                        arrays[array].at[pl.ds(first, size), :],
                        held.at[t, pl.ds(start, size), :],
                        piece_sems.at[sum(len(c) for c in copies)],
                    )
                )

        def panel_copy(t, i):
            k = terms[t][0]
            return pltpu.make_async_copy(
                panels.at[pl.ds(i * tile, tile), pl.ds(k * NB, NB)], panels_here.at[t, i], sems.at[t, i]
            )

        def current_copy(i):
            at = pl.ds(i * tile, tile)
            return pltpu.make_async_copy(current.at[at, :], current_here.at[at, :], sems.at[len(terms), i])

        def load(t, i):
            if i == 0:
                for copy in copies[t]:
                    copy.start()
            if near_panels[t] is None:
                panel_copy(t, i).start()
            if t == 0:
                current_copy(i).start()

        order = [(t, i) for i in range(rows // tile) for t in range(len(terms))]
        in_flight = max(IN_FLIGHT, len(terms))
        for t, i in order[:in_flight]:
            load(t, i)
        sent = []
        for n, (t, i) in enumerate(order):
            at = pl.ds(i * tile, tile)
            if i == 0:
                for copy in copies[t]:
                    copy.wait()
            if t == 0:
                current_copy(i).wait()
                value = current_here[at, :]
            if near_panels[t] is None:
                panel_copy(t, i).wait()
                panel = panels_here[t, i]
            else:
                if part_of_block[t]:
                    sizes = [size for _, _, size, _ in terms[t][1]]
                    panel = jnp.concatenate(
                        [near_panels[t][at, pl.ds(start, size)] for start, size in zip(places[t], sizes)], axis=1
                    )
                else:
                    panel = near_panels[t][at, :]
            if n + in_flight < len(order):
                load(*order[n + in_flight])
            product = jnp.dot(panel, held[t, : panel.shape[1]], preferred_element_type=jnp.float32)
            k, fresh = terms[t][0], terms[t][3]
            less = value - product
            if not fresh:
                less = jnp.where((here.block > k) & (here.block < STEPS), value, less)
            value = jnp.where(here.block == k, product if fresh else value + product, less)
            if t < len(terms) - 1:
                continue
            for o, (dtype, first, size, far) in enumerate(outs):
                low, high = max(first, i * tile), min(first + size, (i + 1) * tile)
                if low < high:
                    part = value[low - i * tile : high - i * tile].astype(dtype)
                    if far:
                        current_here[at, :] = part
                        sent.append(pltpu.make_async_copy(current_here.at[at, :], results[o].at[at, :], out_sems.at[i]))
                        sent[-1].start()
                    else:
                        results[o][pl.ds(low - first, high - low), :] = part
        for out in sent:
            out.wait()

    if only is None:
        work()
    else:
        pl.when(here.block == only)(work)
    for block, array in handed:

        def hand(array=array):
            copies = [
                pltpu.make_async_copy(arrays[array].at[pl.ds(first, size), :], results[o], piece_sems.at[o])
                for o, (_, first, size, _) in enumerate(outs)
            ]
            for copy in copies:
                copy.start()
            for copy in copies:
                copy.wait()

        pl.when(here.block == block)(hand)


def steps(current, factor_panels, terms, outs, where_am_i, only=None, handed=()):
    rows, scenarios = current.shape
    arrays = []

    def index(array):
        for i, other in enumerate(arrays):
            if other is array:
                return i
        arrays.append(array)
        return len(arrays) - 1

    plan = tuple(
        (k, tuple((index(array), first, size, place) for array, first, size, place in pieces), None if near is None else 0, fresh)
        for k, pieces, near, fresh in terms
    )
    near_panels = [near for _, _, near, _ in terms if near is not None]
    handed = tuple((block, index(array)) for block, array in handed)
    n_terms = len(terms)
    tile = min(NEAR_TILE if near_panels else TILE, rows)
    n_pieces = max(sum(len(pieces) for _, pieces, _, _ in terms), len(outs))
    n_far = max(n_terms - len(near_panels), 1)
    assert not near_panels or len(near_panels) == n_terms
    anywhere = pl.BlockSpec(memory_space=pl.ANY)
    return pl.pallas_call(
        functools.partial(step_kernel, plan, handed, len(arrays), tuple(outs), where_am_i, only),
        in_specs=[anywhere] * (1 if near_panels else 2)
        + [pl.BlockSpec(memory_space=pltpu.VMEM)] * len(near_panels)
        + [anywhere] * len(arrays),
        out_specs=[anywhere if out[3] else pl.BlockSpec(memory_space=pltpu.VMEM) for out in outs],
        out_shape=[jax.ShapeDtypeStruct((size, scenarios), dtype) for dtype, _, size, _ in outs],
        scratch_shapes=[
            pltpu.VMEM((rows, scenarios), jnp.float32),
            pltpu.VMEM((n_far, 1 if near_panels else rows // tile, 16 if near_panels else tile, NB), jnp.bfloat16),
            pltpu.VMEM((n_terms, NB, scenarios), jnp.bfloat16),
            pltpu.SemaphoreType.DMA((n_terms + 1, rows // tile)),
            pltpu.SemaphoreType.DMA((n_pieces,)),
            pltpu.SemaphoreType.DMA((rows // tile,)),
        ],
        compiler_params=pltpu.CompilerParams(vmem_limit_bytes=(28 if near_panels else 48) * MIB),
        cost_estimate=pl.CostEstimate(
            flops=2 * rows * NB * scenarios * n_terms,
            bytes_accessed=8 * rows * scenarios,
            transcendentals=0,
        ),
    )(current, *([] if near_panels else [factor_panels]), *near_panels, *arrays)


def near_kernel(k, panels, out, sems):
    parts = sems.shape[0]
    rows = out.shape[0] // parts
    copies = []
    for i in range(parts):
        at = pl.ds(i * rows, rows)
        copies.append(pltpu.make_async_copy(panels.at[at, pl.ds(k * NB, NB)], out.at[at, :], sems.at[i]))
        copies[-1].start()
    for copy in copies:
        copy.wait()


def near_panel(factor_panels, k):
    rows = factor_panels.shape[0]
    return pl.pallas_call(
        functools.partial(near_kernel, k),
        in_specs=[pl.BlockSpec(memory_space=pl.ANY)],
        out_specs=pl.BlockSpec(memory_space=pl.ANY),
        out_shape=pltpu.VMEM((rows, NB), jnp.bfloat16),
        scratch_shapes=[pltpu.SemaphoreType.DMA((4,))],
        compiler_params=pltpu.CompilerParams(vmem_limit_bytes=44 * MIB),
        cost_estimate=pl.CostEstimate(flops=0, bytes_accessed=1, transcendentals=0),
    )(factor_panels)


def make_on_device(n_row, n_col):
    def on_device(rhs_scen, factor_panels):
        rows_here = factor_panels.shape[0]
        lanes = NB // rows_here
        planes = n_col // lanes
        n_y = n_row // CORES
        members = n_row * lanes
        where_am_i = functools.partial(Place, n_col, lanes)
        here = where_am_i()
        core, plane = here.core, here.plane

        def device(y, core, plane, lane):
            return (y * CORES + core) * n_col + plane * lanes + lane

        def send(value, pairs):
            return lax.ppermute(value, AXES, pairs)

        def run(current, terms, outs, only=None, handed=()):
            return steps(current, factor_panels, terms, outs, where_am_i, only, handed)

        def ahead(own, k):
            return [
                send(own, [(device(0, 0, k, (m + d) % lanes), device(0, 0, k + 1, m)) for m in range(lanes)])
                for d in range(lanes)
            ]

        along_x = [(0, d) for d in range(1, lanes)]
        along_y = [(d, 0) for d in range(1, n_y)]
        first_0, first_1 = along_x + along_y, along_y + along_x
        across = [(dy, dm) for dy, _ in along_y for _, dm in along_x]
        offsets = [((0, 0), (0, 0)), *zip(first_0, first_1), *zip(across, across)]

        def plane_gather(value):
            def pairs(c, step):
                return [
                    (device((t + step[0]) % n_y, c, z, (m + step[1]) % lanes), device(t, c, z, m))
                    for t in range(n_y) for z in range(planes) for m in range(lanes)
                ]

            got = [send(value, pairs(0, a) + pairs(1, b)) for a, b in zip(first_0, first_1)]
            last = []
            for dy, dm in across:
                a, b = first_0.index((dy, 0)), first_1.index((0, dm))
                payload = got[a] if a == b else jnp.where(core == 0, got[a], got[b])
                last.append(send(payload, pairs(0, (0, dm)) + pairs(1, (dy, 0))))
            return jnp.concatenate([value, *got], axis=0), jnp.concatenate(last, axis=0)

        def core_exchange(value):
            pairs = [
                (device(t, 1 - c, z, m), device(t, c, z, m))
                for t in range(n_y) for c in range(CORES) for z in range(planes) for m in range(lanes)
            ]
            return send(value, pairs)

        def gathered_pieces(array, own, first, size, stride, offsets, number):
            def place(offset, own, at):
                c = at.core if own else 1 - at.core
                a, b = (number((at.y + dy) % n_y, c, (at.lane + dm) % lanes) for dy, dm in offset)
                return a if offset[0] == offset[1] else jnp.where(c == 0, a, b)

            return [
                (array, i * stride + first, size, functools.partial(place, offset, own))
                for i, offset in enumerate(offsets)
            ]

        def lane_pieces(parts):
            return [
                (part, 0, rows_here, functools.partial(lambda d, at: (at.lane + d) % lanes, d))
                for d, part in enumerate(parts)
            ]

        f32_rows = (jnp.float32, 0, rows_here, False)
        own_rows = (jnp.bfloat16, 0, rows_here, False)
        cut = rows_here // n_row
        own_cuts = [(jnp.bfloat16, t * cut, cut, False) for t in range(n_row)]

        extra = NB // members
        first = rhs_scen.reshape(rhs_scen.shape[0], -1, extra)[:, :members].reshape(-1, n_row, 1, lanes, extra)
        first = jnp.broadcast_to(first, (first.shape[0], n_row, planes, lanes, extra))
        first = first.reshape(first.shape[0], n_row * n_col, extra)
        outgoing = jnp.concatenate(
            [rhs_scen.reshape(rhs_scen.shape[0], n_row * n_col, rows_here), first], axis=2
        )
        regrouped = lax.all_to_all(outgoing, AXES, split_axis=1, concat_axis=0, tiled=True)
        regrouped = regrouped.reshape(-1, rows_here + extra)
        current = jnp.transpose(regrouped[:, :rows_here]).astype(jnp.float32)
        whole = jnp.concatenate(plane_gather(jnp.transpose(regrouped[:, rows_here:])), axis=0)
        near0 = near_panel(after(factor_panels, whole), 0)
        pieces = [
            piece
            for array, own in ((whole, True), (core_exchange(whole), False))
            for piece in gathered_pieces(
                array, own, 0, extra, extra, offsets, lambda y, c, m: (y * CORES + c) * lanes + m
            )
        ]
        current, own1 = run(current, [(0, pieces, near0, True)], [f32_rows, own_rows])

        hop1 = ahead(own1, 1)
        near1 = near_panel(after(factor_panels, own1), 1)
        start1 = after(own1, hop1[0], near1)
        at_3 = [
            send(start1, [(device(0, 0, 1, (m + d) % lanes), device(0, 0, 3, m)) for m in range(lanes)])
            for d in range(lanes)
        ]
        (own2,) = run(current, [(1, lane_pieces(hop1), near1, True)], [own_rows], 2)
        hop2 = ahead(own2, 2)
        near2 = near_panel(after(factor_panels, own2), 2)
        (chained,) = run(after(current, near2), [(1, lane_pieces(at_3), near1, True)], [f32_rows], 3)
        cuts = run(chained, [(2, lane_pieces(hop2), near2, True)], own_cuts, 3, [(1, own1), (2, own2)])

        piece = cuts[0]
        for t in range(1, n_row):
            pairs = [
                (device(0, 0, k, m), device(t // CORES, t % CORES, k, m)) for k in range(1, STEPS) for m in range(lanes)
            ]
            piece = jnp.where(here.y * CORES + core == t, send(cuts[t], pairs), piece)
        got = [
            send(
                piece,
                [
                    (device(t, c, k, m), device(t, c, (k + d) % planes, m))
                    for k in range(1, STEPS) for t in range(n_y) for c in range(CORES) for m in range(lanes)
                ],
            )
            for d in range(1, planes)
        ]
        three = []
        for k in range(1, STEPS):
            value = piece
            for d in range(1, planes):
                value = jnp.where(plane == (k + d) % planes, got[d - 1], value)
            three.append(value)
        near3 = near_panel(after(factor_panels, cuts[0]), 3)
        most, last = plane_gather(after(jnp.concatenate(three, axis=0), near3))
        n_most = len(offsets) - len(across)

        def terms(fresh, *arrays):
            return [
                (
                    k,
                    [
                        piece
                        for array, own, start, count in arrays
                        for piece in gathered_pieces(
                            array, own, (k - 1) * cut, cut, (STEPS - 1) * cut, offsets[start : start + count],
                            lambda y, c, m: m * n_row + y * CORES + c,
                        )
                    ],
                    near,
                    fresh,
                )
                for k, near in ((1, near1), (2, near2), (3, near3))
            ]

        (current,) = run(current, terms(True, (most, True, 0, n_most)), [f32_rows])
        whole = after(jnp.concatenate([most, last], axis=0), current)
        other = core_exchange(whole)
        (current,) = run(current, terms(False, (last, True, n_most, len(across))), [f32_rows])
        (out,) = run(current, terms(False, (other, False, 0, len(offsets))), [(jnp.float32, 0, rows_here, True)])
        return out

    return on_device


def solution(mesh):
    placed = (P(AXES, None), P(AXES, None))
    on_device = make_on_device(mesh.shape["row"], mesh.shape["col"])
    return jax.shard_map(
        on_device, mesh=mesh, in_specs=placed, out_specs=P(AXES, None), check_vma=False
    )
```

```python
import functools

import jax
import jax.numpy as jnp
from jax import lax
from jax.experimental import pallas as pl
from jax.experimental.pallas import tpu as pltpu
from jax.sharding import PartitionSpec as P

NB = 2048
STEPS = 4
AXES = ("row", "col")
CORES = 2
TILE = 256
NEAR_TILE = 1024
IN_FLIGHT = 3
MIB = 1024 * 1024


def after(value, *others):
    return lax.optimization_barrier((value, *others))[0]


class Place:
    def __init__(self, n_col, lanes):
        row, col = lax.axis_index("row"), lax.axis_index("col")
        self.y, self.core = row // CORES, row % CORES
        self.plane, self.lane = col // lanes, col % lanes
        self.block = (row * n_col + col) // lanes


def step_kernel(terms, handed, n_arrays, outs, where_am_i, only, *refs):
    refs = list(refs)
    current = refs.pop(0)
    panels = refs.pop(0) if any(near is None for _, _, near, _ in terms) else None
    near_panels = [None if near is None else refs.pop(0) for _, _, near, _ in terms]
    arrays, refs = refs[:n_arrays], refs[n_arrays:]
    results, refs = refs[: len(outs)], refs[len(outs) :]
    current_here, panels_here, held, sems, piece_sems, out_sems = refs
    rows = current.shape[0]
    tile = min(NEAR_TILE if near_panels[0] is not None else TILE, rows)
    here = where_am_i()

    def work():
        copies = [[] for _ in terms]
        places, part_of_block = [], []
        for t, (_, pieces, _, _) in enumerate(terms):
            places.append([pl.multiple_of(place(here) * size, size) for _, _, size, place in pieces])
            part_of_block.append(sum(size for _, _, size, _ in pieces) < NB)
            for j, (array, first, size, _) in enumerate(pieces):
                start = j * size if part_of_block[t] else places[t][j]
                copies[t].append(
                    pltpu.make_async_copy(
                        arrays[array].at[pl.ds(first, size), :],
                        held.at[t, pl.ds(start, size), :],
                        piece_sems.at[sum(len(c) for c in copies)],
                    )
                )

        def panel_copy(t, i):
            k = terms[t][0]
            return pltpu.make_async_copy(
                panels.at[pl.ds(i * tile, tile), pl.ds(k * NB, NB)], panels_here.at[t, i], sems.at[t, i]
            )

        def current_copy(i):
            at = pl.ds(i * tile, tile)
            return pltpu.make_async_copy(current.at[at, :], current_here.at[at, :], sems.at[len(terms), i])

        def load(t, i):
            if i == 0:
                for copy in copies[t]:
                    copy.start()
            if near_panels[t] is None:
                panel_copy(t, i).start()
            if t == 0:
                current_copy(i).start()

        order = [(t, i) for i in range(rows // tile) for t in range(len(terms))]
        in_flight = max(IN_FLIGHT, len(terms))
        for t, i in order[:in_flight]:
            load(t, i)
        sent = []
        for n, (t, i) in enumerate(order):
            at = pl.ds(i * tile, tile)
            if i == 0:
                for copy in copies[t]:
                    copy.wait()
            if t == 0:
                current_copy(i).wait()
                value = current_here[at, :]
            if near_panels[t] is None:
                panel_copy(t, i).wait()
                panel = panels_here[t, i]
            else:
                if part_of_block[t]:
                    sizes = [size for _, _, size, _ in terms[t][1]]
                    panel = jnp.concatenate(
                        [near_panels[t][at, pl.ds(start, size)] for start, size in zip(places[t], sizes)], axis=1
                    )
                else:
                    panel = near_panels[t][at, :]
            if n + in_flight < len(order):
                load(*order[n + in_flight])
            product = jnp.dot(panel, held[t, : panel.shape[1]], preferred_element_type=jnp.float32)
            k, fresh = terms[t][0], terms[t][3]
            less = value - product
            if not fresh:
                less = jnp.where((here.block > k) & (here.block < STEPS), value, less)
            value = jnp.where(here.block == k, product if fresh else value + product, less)
            if t < len(terms) - 1:
                continue
            for o, (dtype, first, size, far) in enumerate(outs):
                low, high = max(first, i * tile), min(first + size, (i + 1) * tile)
                if low < high:
                    part = value[low - i * tile : high - i * tile].astype(dtype)
                    if far:
                        current_here[at, :] = part
                        sent.append(pltpu.make_async_copy(current_here.at[at, :], results[o].at[at, :], out_sems.at[i]))
                        sent[-1].start()
                    else:
                        results[o][pl.ds(low - first, high - low), :] = part
        for out in sent:
            out.wait()

    if only is None:
        work()
    else:
        pl.when(here.block == only)(work)
    for block, array in handed:

        def hand(array=array):
            copies = [
                pltpu.make_async_copy(arrays[array].at[pl.ds(first, size), :], results[o], piece_sems.at[o])
                for o, (_, first, size, _) in enumerate(outs)
            ]
            for copy in copies:
                copy.start()
            for copy in copies:
                copy.wait()

        pl.when(here.block == block)(hand)


def steps(current, factor_panels, terms, outs, where_am_i, only=None, handed=()):
    rows, scenarios = current.shape
    arrays = []

    def index(array):
        for i, other in enumerate(arrays):
            if other is array:
                return i
        arrays.append(array)
        return len(arrays) - 1

    plan = tuple(
        (k, tuple((index(array), first, size, place) for array, first, size, place in pieces), None if near is None else 0, fresh)
        for k, pieces, near, fresh in terms
    )
    near_panels = [near for _, _, near, _ in terms if near is not None]
    handed = tuple((block, index(array)) for block, array in handed)
    n_terms = len(terms)
    tile = min(NEAR_TILE if near_panels else TILE, rows)
    n_pieces = max(sum(len(pieces) for _, pieces, _, _ in terms), len(outs))
    n_far = max(n_terms - len(near_panels), 1)
    assert not near_panels or len(near_panels) == n_terms
    anywhere = pl.BlockSpec(memory_space=pl.ANY)
    return pl.pallas_call(
        functools.partial(step_kernel, plan, handed, len(arrays), tuple(outs), where_am_i, only),
        in_specs=[anywhere] * (1 if near_panels else 2)
        + [pl.BlockSpec(memory_space=pltpu.VMEM)] * len(near_panels)
        + [anywhere] * len(arrays),
        out_specs=[anywhere if out[3] else pl.BlockSpec(memory_space=pltpu.VMEM) for out in outs],
        out_shape=[jax.ShapeDtypeStruct((size, scenarios), dtype) for dtype, _, size, _ in outs],
        scratch_shapes=[
            pltpu.VMEM((rows, scenarios), jnp.float32),
            pltpu.VMEM((n_far, 1 if near_panels else rows // tile, 16 if near_panels else tile, NB), jnp.bfloat16),
            pltpu.VMEM((n_terms, NB, scenarios), jnp.bfloat16),
            pltpu.SemaphoreType.DMA((n_terms + 1, rows // tile)),
            pltpu.SemaphoreType.DMA((n_pieces,)),
            pltpu.SemaphoreType.DMA((rows // tile,)),
        ],
        compiler_params=pltpu.CompilerParams(vmem_limit_bytes=(28 if near_panels else 48) * MIB),
        cost_estimate=pl.CostEstimate(
            flops=2 * rows * NB * scenarios * n_terms,
            bytes_accessed=8 * rows * scenarios,
            transcendentals=0,
        ),
    )(current, *([] if near_panels else [factor_panels]), *near_panels, *arrays)


def near_kernel(k, panels, out, sems):
    parts = sems.shape[0]
    rows = out.shape[0] // parts
    copies = []
    for i in range(parts):
        at = pl.ds(i * rows, rows)
        copies.append(pltpu.make_async_copy(panels.at[at, pl.ds(k * NB, NB)], out.at[at, :], sems.at[i]))
        copies[-1].start()
    for copy in copies:
        copy.wait()


def near_panel(factor_panels, k):
    rows = factor_panels.shape[0]
    return pl.pallas_call(
        functools.partial(near_kernel, k),
        in_specs=[pl.BlockSpec(memory_space=pl.ANY)],
        out_specs=pl.BlockSpec(memory_space=pl.ANY),
        out_shape=pltpu.VMEM((rows, NB), jnp.bfloat16),
        scratch_shapes=[pltpu.SemaphoreType.DMA((4,))],
        compiler_params=pltpu.CompilerParams(vmem_limit_bytes=44 * MIB),
        cost_estimate=pl.CostEstimate(flops=0, bytes_accessed=1, transcendentals=0),
    )(factor_panels)


def make_on_device(n_row, n_col):
    def on_device(rhs_scen, factor_panels):
        rows_here = factor_panels.shape[0]
        lanes = NB // rows_here
        planes = n_col // lanes
        n_y = n_row // CORES
        members = n_row * lanes
        where_am_i = functools.partial(Place, n_col, lanes)
        here = where_am_i()
        core, plane = here.core, here.plane

        def device(y, core, plane, lane):
            return (y * CORES + core) * n_col + plane * lanes + lane

        def send(value, pairs):
            return lax.ppermute(value, AXES, pairs)

        def run(current, terms, outs, only=None, handed=()):
            return steps(current, factor_panels, terms, outs, where_am_i, only, handed)

        def ahead(own, k):
            return [
                send(own, [(device(0, 0, k, (m + d) % lanes), device(0, 0, k + 1, m)) for m in range(lanes)])
                for d in range(lanes)
            ]

        along_x = [(0, d) for d in range(1, lanes)]
        along_y = [(d, 0) for d in range(1, n_y)]
        first_0, first_1 = along_x + along_y, along_y + along_x
        across = [(dy, dm) for dy, _ in along_y for _, dm in along_x]
        offsets = [((0, 0), (0, 0)), *zip(first_0, first_1), *zip(across, across)]

        def plane_gather(value):
            def pairs(c, step):
                return [
                    (device((t + step[0]) % n_y, c, z, (m + step[1]) % lanes), device(t, c, z, m))
                    for t in range(n_y) for z in range(planes) for m in range(lanes)
                ]

            got = [send(value, pairs(0, a) + pairs(1, b)) for a, b in zip(first_0, first_1)]
            last = []
            for dy, dm in across:
                a, b = first_0.index((dy, 0)), first_1.index((0, dm))
                payload = got[a] if a == b else jnp.where(core == 0, got[a], got[b])
                last.append(send(payload, pairs(0, (0, dm)) + pairs(1, (dy, 0))))
            return jnp.concatenate([value, *got], axis=0), jnp.concatenate(last, axis=0)

        def core_exchange(value):
            pairs = [
                (device(t, 1 - c, z, m), device(t, c, z, m))
                for t in range(n_y) for c in range(CORES) for z in range(planes) for m in range(lanes)
            ]
            return send(value, pairs)

        def gathered_pieces(array, own, first, size, stride, offsets, number):
            def place(offset, own, at):
                c = at.core if own else 1 - at.core
                a, b = (number((at.y + dy) % n_y, c, (at.lane + dm) % lanes) for dy, dm in offset)
                return a if offset[0] == offset[1] else jnp.where(c == 0, a, b)

            return [
                (array, i * stride + first, size, functools.partial(place, offset, own))
                for i, offset in enumerate(offsets)
            ]

        def lane_pieces(parts):
            return [
                (part, 0, rows_here, functools.partial(lambda d, at: (at.lane + d) % lanes, d))
                for d, part in enumerate(parts)
            ]

        f32_rows = (jnp.float32, 0, rows_here, False)
        own_rows = (jnp.bfloat16, 0, rows_here, False)
        cut = rows_here // n_row
        own_cuts = [(jnp.bfloat16, t * cut, cut, False) for t in range(n_row)]

        extra = NB // members
        first = rhs_scen.reshape(rhs_scen.shape[0], -1, extra)[:, :members].reshape(-1, n_row, 1, lanes, extra)
        first = jnp.broadcast_to(first, (first.shape[0], n_row, planes, lanes, extra))
        first = first.reshape(first.shape[0], n_row * n_col, extra)
        outgoing = jnp.concatenate(
            [rhs_scen.reshape(rhs_scen.shape[0], n_row * n_col, rows_here), first], axis=2
        )
        regrouped = lax.all_to_all(outgoing, AXES, split_axis=1, concat_axis=0, tiled=True)
        regrouped = regrouped.reshape(-1, rows_here + extra)
        current = jnp.transpose(regrouped[:, :rows_here]).astype(jnp.float32)
        whole = jnp.concatenate(plane_gather(jnp.transpose(regrouped[:, rows_here:])), axis=0)
        near0 = near_panel(after(factor_panels, whole), 0)
        pieces = [
            piece
            for array, own in ((whole, True), (core_exchange(whole), False))
            for piece in gathered_pieces(
                array, own, 0, extra, extra, offsets, lambda y, c, m: (y * CORES + c) * lanes + m
            )
        ]
        current, own1 = run(current, [(0, pieces, near0, True)], [f32_rows, own_rows])

        hop1 = ahead(own1, 1)
        near1 = near_panel(after(factor_panels, own1), 1)
        start1 = after(own1, hop1[0], near1)
        at_3 = [
            send(start1, [(device(0, 0, 1, (m + d) % lanes), device(0, 0, 3, m)) for m in range(lanes)])
            for d in range(lanes)
        ]
        (own2,) = run(current, [(1, lane_pieces(hop1), near1, True)], [own_rows], 2)
        hop2 = ahead(own2, 2)
        near2 = near_panel(after(factor_panels, own2), 2)
        (chained,) = run(after(current, near2), [(1, lane_pieces(at_3), near1, True)], [f32_rows], 3)
        cuts = run(chained, [(2, lane_pieces(hop2), near2, True)], own_cuts, 3, [(1, own1), (2, own2)])

        piece = cuts[0]
        for t in range(1, n_row):
            pairs = [
                (device(0, 0, k, m), device(t // CORES, t % CORES, k, m)) for k in range(1, STEPS) for m in range(lanes)
            ]
            piece = jnp.where(here.y * CORES + core == t, send(cuts[t], pairs), piece)
        got = [
            send(
                piece,
                [
                    (device(t, c, k, m), device(t, c, (k + d) % planes, m))
                    for k in range(1, STEPS) for t in range(n_y) for c in range(CORES) for m in range(lanes)
                ],
            )
            for d in range(1, planes)
        ]
        three = []
        for k in range(1, STEPS):
            value = piece
            for d in range(1, planes):
                value = jnp.where(plane == (k + d) % planes, got[d - 1], value)
            three.append(value)
        near3 = near_panel(after(factor_panels, cuts[0]), 3)
        most, last = plane_gather(after(jnp.concatenate(three, axis=0), near3))
        n_most = len(offsets) - len(across)

        def terms(fresh, *arrays):
            return [
                (
                    k,
                    [
                        piece
                        for array, own, start, count in arrays
                        for piece in gathered_pieces(
                            array, own, (k - 1) * cut, cut, (STEPS - 1) * cut, offsets[start : start + count],
                            lambda y, c, m: m * n_row + y * CORES + c,
                        )
                    ],
                    near,
                    fresh,
                )
                for k, near in ((1, near1), (2, near2), (3, near3))
            ]

        (current,) = run(current, terms(True, (most, True, 0, n_most)), [f32_rows])
        whole = after(jnp.concatenate([most, last], axis=0), current)
        other = core_exchange(whole)
        (current,) = run(current, terms(False, (last, True, n_most, len(across))), [f32_rows])
        (out,) = run(current, terms(False, (other, False, 0, len(offsets))), [(jnp.float32, 0, rows_here, True)])
        return out

    return on_device


def solution(mesh):
    placed = (P(AXES, None), P(AXES, None))
    on_device = make_on_device(mesh.shape["row"], mesh.shape["col"])
    return jax.shard_map(
        on_device, mesh=mesh, in_specs=placed, out_specs=P(AXES, None), check_vma=False
    )
```

```python
import functools

import jax
import jax.numpy as jnp
from jax import lax
from jax.experimental import pallas as pl
from jax.experimental.pallas import tpu as pltpu
from jax.sharding import PartitionSpec as P

NB = 2048
STEPS = 4
AXES = ("row", "col")
CORES = 2
TILE = 256
NEAR_TILE = 1024
IN_FLIGHT = 3
MIB = 1024 * 1024


def after(value, *others):
    return lax.optimization_barrier((value, *others))[0]


class Place:
    def __init__(self, n_col, lanes):
        row, col = lax.axis_index("row"), lax.axis_index("col")
        self.y, self.core = row // CORES, row % CORES
        self.plane, self.lane = col // lanes, col % lanes
        self.block = (row * n_col + col) // lanes


def step_kernel(terms, handed, n_arrays, outs, where_am_i, only, *refs):
    refs = list(refs)
    current = refs.pop(0)
    panels = refs.pop(0) if any(near is None for _, _, near, _ in terms) else None
    near_panels = [None if near is None else refs.pop(0) for _, _, near, _ in terms]
    arrays, refs = refs[:n_arrays], refs[n_arrays:]
    results, refs = refs[: len(outs)], refs[len(outs) :]
    current_here, panels_here, held, sems, piece_sems, out_sems = refs
    rows = current.shape[0]
    tile = min(NEAR_TILE if near_panels[0] is not None else TILE, rows)
    here = where_am_i()

    def work():
        copies = [[] for _ in terms]
        places, part_of_block = [], []
        for t, (_, pieces, _, _) in enumerate(terms):
            places.append([pl.multiple_of(place(here) * size, size) for _, _, size, place in pieces])
            part_of_block.append(sum(size for _, _, size, _ in pieces) < NB)
            for j, (array, first, size, _) in enumerate(pieces):
                start = j * size if part_of_block[t] else places[t][j]
                copies[t].append(
                    pltpu.make_async_copy(
                        arrays[array].at[pl.ds(first, size), :],
                        held.at[t, pl.ds(start, size), :],
                        piece_sems.at[sum(len(c) for c in copies)],
                    )
                )

        def panel_copy(t, i):
            k = terms[t][0]
            return pltpu.make_async_copy(
                panels.at[pl.ds(i * tile, tile), pl.ds(k * NB, NB)], panels_here.at[t, i], sems.at[t, i]
            )

        def current_copy(i):
            at = pl.ds(i * tile, tile)
            return pltpu.make_async_copy(current.at[at, :], current_here.at[at, :], sems.at[len(terms), i])

        def load(t, i):
            if i == 0:
                for copy in copies[t]:
                    copy.start()
            if near_panels[t] is None:
                panel_copy(t, i).start()
            if t == 0:
                current_copy(i).start()

        order = [(t, i) for i in range(rows // tile) for t in range(len(terms))]
        in_flight = max(IN_FLIGHT, len(terms))
        for t, i in order[:in_flight]:
            load(t, i)
        sent = []
        for n, (t, i) in enumerate(order):
            at = pl.ds(i * tile, tile)
            if i == 0:
                for copy in copies[t]:
                    copy.wait()
            if t == 0:
                current_copy(i).wait()
                value = current_here[at, :]
            if near_panels[t] is None:
                panel_copy(t, i).wait()
                panel = panels_here[t, i]
            else:
                if part_of_block[t]:
                    sizes = [size for _, _, size, _ in terms[t][1]]
                    panel = jnp.concatenate(
                        [near_panels[t][at, pl.ds(start, size)] for start, size in zip(places[t], sizes)], axis=1
                    )
                else:
                    panel = near_panels[t][at, :]
            if n + in_flight < len(order):
                load(*order[n + in_flight])
            product = jnp.dot(panel, held[t, : panel.shape[1]], preferred_element_type=jnp.float32)
            k, fresh = terms[t][0], terms[t][3]
            less = value - product
            if not fresh:
                less = jnp.where((here.block > k) & (here.block < STEPS), value, less)
            value = jnp.where(here.block == k, product if fresh else value + product, less)
            if t < len(terms) - 1:
                continue
            for o, (dtype, first, size, far) in enumerate(outs):
                low, high = max(first, i * tile), min(first + size, (i + 1) * tile)
                if low < high:
                    part = value[low - i * tile : high - i * tile].astype(dtype)
                    if far:
                        current_here[at, :] = part
                        sent.append(pltpu.make_async_copy(current_here.at[at, :], results[o].at[at, :], out_sems.at[i]))
                        sent[-1].start()
                    else:
                        results[o][pl.ds(low - first, high - low), :] = part
        for out in sent:
            out.wait()

    if only is None:
        work()
    else:
        pl.when(here.block == only)(work)
    for block, array in handed:

        def hand(array=array):
            copies = [
                pltpu.make_async_copy(arrays[array].at[pl.ds(first, size), :], results[o], piece_sems.at[o])
                for o, (_, first, size, _) in enumerate(outs)
            ]
            for copy in copies:
                copy.start()
            for copy in copies:
                copy.wait()

        pl.when(here.block == block)(hand)


def steps(current, factor_panels, terms, outs, where_am_i, only=None, handed=()):
    rows, scenarios = current.shape
    arrays = []

    def index(array):
        for i, other in enumerate(arrays):
            if other is array:
                return i
        arrays.append(array)
        return len(arrays) - 1

    plan = tuple(
        (k, tuple((index(array), first, size, place) for array, first, size, place in pieces), None if near is None else 0, fresh)
        for k, pieces, near, fresh in terms
    )
    near_panels = [near for _, _, near, _ in terms if near is not None]
    handed = tuple((block, index(array)) for block, array in handed)
    n_terms = len(terms)
    tile = min(NEAR_TILE if near_panels else TILE, rows)
    n_pieces = max(sum(len(pieces) for _, pieces, _, _ in terms), len(outs))
    n_far = max(n_terms - len(near_panels), 1)
    assert not near_panels or len(near_panels) == n_terms
    anywhere = pl.BlockSpec(memory_space=pl.ANY)
    return pl.pallas_call(
        functools.partial(step_kernel, plan, handed, len(arrays), tuple(outs), where_am_i, only),
        in_specs=[anywhere] * (1 if near_panels else 2)
        + [pl.BlockSpec(memory_space=pltpu.VMEM)] * len(near_panels)
        + [anywhere] * len(arrays),
        out_specs=[anywhere if out[3] else pl.BlockSpec(memory_space=pltpu.VMEM) for out in outs],
        out_shape=[jax.ShapeDtypeStruct((size, scenarios), dtype) for dtype, _, size, _ in outs],
        scratch_shapes=[
            pltpu.VMEM((rows, scenarios), jnp.float32),
            pltpu.VMEM((n_far, 1 if near_panels else rows // tile, 16 if near_panels else tile, NB), jnp.bfloat16),
            pltpu.VMEM((n_terms, NB, scenarios), jnp.bfloat16),
            pltpu.SemaphoreType.DMA((n_terms + 1, rows // tile)),
            pltpu.SemaphoreType.DMA((n_pieces,)),
            pltpu.SemaphoreType.DMA((rows // tile,)),
        ],
        compiler_params=pltpu.CompilerParams(vmem_limit_bytes=(28 if near_panels else 48) * MIB),
        cost_estimate=pl.CostEstimate(
            flops=2 * rows * NB * scenarios * n_terms,
            bytes_accessed=8 * rows * scenarios,
            transcendentals=0,
        ),
    )(current, *([] if near_panels else [factor_panels]), *near_panels, *arrays)


def near_kernel(k, panels, out, sems):
    parts = sems.shape[0]
    rows = out.shape[0] // parts
    copies = []
    for i in range(parts):
        at = pl.ds(i * rows, rows)
        copies.append(pltpu.make_async_copy(panels.at[at, pl.ds(k * NB, NB)], out.at[at, :], sems.at[i]))
        copies[-1].start()
    for copy in copies:
        copy.wait()


def near_panel(factor_panels, k):
    rows = factor_panels.shape[0]
    return pl.pallas_call(
        functools.partial(near_kernel, k),
        in_specs=[pl.BlockSpec(memory_space=pl.ANY)],
        out_specs=pl.BlockSpec(memory_space=pl.ANY),
        out_shape=pltpu.VMEM((rows, NB), jnp.bfloat16),
        scratch_shapes=[pltpu.SemaphoreType.DMA((4,))],
        compiler_params=pltpu.CompilerParams(vmem_limit_bytes=44 * MIB),
        cost_estimate=pl.CostEstimate(flops=0, bytes_accessed=1, transcendentals=0),
    )(factor_panels)


def make_on_device(n_row, n_col):
    def on_device(rhs_scen, factor_panels):
        rows_here = factor_panels.shape[0]
        lanes = NB // rows_here
        planes = n_col // lanes
        n_y = n_row // CORES
        members = n_row * lanes
        where_am_i = functools.partial(Place, n_col, lanes)
        here = where_am_i()
        core, plane = here.core, here.plane

        def device(y, core, plane, lane):
            return (y * CORES + core) * n_col + plane * lanes + lane

        def send(value, pairs):
            return lax.ppermute(value, AXES, pairs)

        def run(current, terms, outs, only=None, handed=()):
            return steps(current, factor_panels, terms, outs, where_am_i, only, handed)

        def ahead(own, k):
            return [
                send(own, [(device(0, 0, k, (m + d) % lanes), device(0, 0, k + 1, m)) for m in range(lanes)])
                for d in range(lanes)
            ]

        along_x = [(0, d) for d in range(1, lanes)]
        along_y = [(d, 0) for d in range(1, n_y)]
        first_0, first_1 = along_x + along_y, along_y + along_x
        across = [(dy, dm) for dy, _ in along_y for _, dm in along_x]
        offsets = [((0, 0), (0, 0)), *zip(first_0, first_1), *zip(across, across)]

        def plane_gather(value):
            def pairs(c, step):
                return [
                    (device((t + step[0]) % n_y, c, z, (m + step[1]) % lanes), device(t, c, z, m))
                    for t in range(n_y) for z in range(planes) for m in range(lanes)
                ]

            got = [send(value, pairs(0, a) + pairs(1, b)) for a, b in zip(first_0, first_1)]
            last = []
            for dy, dm in across:
                a, b = first_0.index((dy, 0)), first_1.index((0, dm))
                payload = got[a] if a == b else jnp.where(core == 0, got[a], got[b])
                last.append(send(payload, pairs(0, (0, dm)) + pairs(1, (dy, 0))))
            return jnp.concatenate([value, *got], axis=0), jnp.concatenate(last, axis=0)

        def core_exchange(value):
            pairs = [
                (device(t, 1 - c, z, m), device(t, c, z, m))
                for t in range(n_y) for c in range(CORES) for z in range(planes) for m in range(lanes)
            ]
            return send(value, pairs)

        def gathered_pieces(array, own, first, size, stride, offsets, number):
            def place(offset, own, at):
                c = at.core if own else 1 - at.core
                a, b = (number((at.y + dy) % n_y, c, (at.lane + dm) % lanes) for dy, dm in offset)
                return a if offset[0] == offset[1] else jnp.where(c == 0, a, b)

            return [
                (array, i * stride + first, size, functools.partial(place, offset, own))
                for i, offset in enumerate(offsets)
            ]

        def lane_pieces(parts):
            return [
                (part, 0, rows_here, functools.partial(lambda d, at: (at.lane + d) % lanes, d))
                for d, part in enumerate(parts)
            ]

        f32_rows = (jnp.float32, 0, rows_here, False)
        own_rows = (jnp.bfloat16, 0, rows_here, False)
        cut = rows_here // n_row
        own_cuts = [(jnp.bfloat16, t * cut, cut, False) for t in range(n_row)]

        extra = NB // members
        first = rhs_scen.reshape(rhs_scen.shape[0], -1, extra)[:, :members].reshape(-1, n_row, 1, lanes, extra)
        first = jnp.broadcast_to(first, (first.shape[0], n_row, planes, lanes, extra))
        first = first.reshape(first.shape[0], n_row * n_col, extra)
        outgoing = jnp.concatenate(
            [rhs_scen.reshape(rhs_scen.shape[0], n_row * n_col, rows_here), first], axis=2
        )
        regrouped = lax.all_to_all(outgoing, AXES, split_axis=1, concat_axis=0, tiled=True)
        regrouped = regrouped.reshape(-1, rows_here + extra)
        current = jnp.transpose(regrouped[:, :rows_here]).astype(jnp.float32)
        whole = jnp.concatenate(plane_gather(jnp.transpose(regrouped[:, rows_here:])), axis=0)
        near0 = near_panel(after(factor_panels, whole), 0)
        pieces = [
            piece
            for array, own in ((whole, True), (core_exchange(whole), False))
            for piece in gathered_pieces(
                array, own, 0, extra, extra, offsets, lambda y, c, m: (y * CORES + c) * lanes + m
            )
        ]
        current, own1 = run(current, [(0, pieces, near0, True)], [f32_rows, own_rows])

        hop1 = ahead(own1, 1)
        near1 = near_panel(after(factor_panels, own1), 1)
        start1 = after(own1, hop1[0], near1)
        at_3 = [
            send(start1, [(device(0, 0, 1, (m + d) % lanes), device(0, 0, 3, m)) for m in range(lanes)])
            for d in range(lanes)
        ]
        (own2,) = run(current, [(1, lane_pieces(hop1), near1, True)], [own_rows], 2)
        hop2 = ahead(own2, 2)
        near2 = near_panel(after(factor_panels, own2), 2)
        (chained,) = run(after(current, near2), [(1, lane_pieces(at_3), near1, True)], [f32_rows], 3)
        cuts = run(chained, [(2, lane_pieces(hop2), near2, True)], own_cuts, 3, [(1, own1), (2, own2)])

        piece = cuts[0]
        for t in range(1, n_row):
            pairs = [
                (device(0, 0, k, m), device(t // CORES, t % CORES, k, m)) for k in range(1, STEPS) for m in range(lanes)
            ]
            piece = jnp.where(here.y * CORES + core == t, send(cuts[t], pairs), piece)
        got = [
            send(
                piece,
                [
                    (device(t, c, k, m), device(t, c, (k + d) % planes, m))
                    for k in range(1, STEPS) for t in range(n_y) for c in range(CORES) for m in range(lanes)
                ],
            )
            for d in range(1, planes)
        ]
        three = []
        for k in range(1, STEPS):
            value = piece
            for d in range(1, planes):
                value = jnp.where(plane == (k + d) % planes, got[d - 1], value)
            three.append(value)
        near3 = near_panel(after(factor_panels, cuts[0]), 3)
        most, last = plane_gather(after(jnp.concatenate(three, axis=0), near3))
        n_most = len(offsets) - len(across)

        def terms(fresh, *arrays):
            return [
                (
                    k,
                    [
                        piece
                        for array, own, start, count in arrays
                        for piece in gathered_pieces(
                            array, own, (k - 1) * cut, cut, (STEPS - 1) * cut, offsets[start : start + count],
                            lambda y, c, m: m * n_row + y * CORES + c,
                        )
                    ],
                    near,
                    fresh,
                )
                for k, near in ((1, near1), (2, near2), (3, near3))
            ]

        other = core_exchange(jnp.concatenate([most, last], axis=0))
        parts = [(most, True, 0, n_most), (last, True, n_most, len(across)), (other, False, 0, len(offsets))]
        (out,) = run(current, terms(True, *parts), [(jnp.float32, 0, rows_here, True)])
        return out

    return on_device


def solution(mesh):
    placed = (P(AXES, None), P(AXES, None))
    on_device = make_on_device(mesh.shape["row"], mesh.shape["col"])
    return jax.shard_map(
        on_device, mesh=mesh, in_specs=placed, out_specs=P(AXES, None), check_vma=False
    )
```
